128 devices in a mesh: tm: 16 (over y, x), units: 8 (over z, core).
Axes of the slice: x: 4, y: 4, z: 4, core: 2. Of those that a mesh axis runs over, the one named last changes fastest.
Arguments:
- trajectory: float32 [16384, 32768], P('tm', 'units'), may hold values from -6 to 6
- block_values: float32 [256, 2, 128, 128], P('units'), may hold values from -0.046875 to 0.046875
- block_index: int32 [256, 2], P('units'), may hold values from 0 to 3, all different within a row
Outputs:
- basis: float32 [16384, 512], P('tm')
- factor: float32 [512, 512], replicated
The draws below stay inside these ranges and needn't reach their ends.
Inputs may be any that keep to these rules, and one draw needn't show every extreme that they name: `block_index`: each row names 2 different column blocks, and every column block is named somewhere.
All inputs are finite; a program needn't handle non-finite values.
Results may differ from the reference program's by a relative error of at most 0.00016.
Values sent between devices are 32-bit elements; how exact they have to be, the bound alone decides.
A program may use at most 192 MiB of HBM per device.

```python
import jax
import jax.numpy as jnp
from jax import lax

UNITS = 32768
BLOCK = 128
KB = 4
SEL = 2
NBLK = 256
TIME = 16384


def level_of(rng, dims, split, low, largest):
    def one(dim, shards_of):
        steps = jax.random.uniform(jax.random.fold_in(jax.random.fold_in(rng, 6), dim), (shards_of,), jnp.float32, low / len(split), largest / len(split))
        return jnp.repeat(jnp.exp(steps), dims[dim] // shards_of).reshape((-1,) + (1,) * (len(dims) - dim - 1))

    factor_of = one(*split[0])
    for cut in split[1:]:
        factor_of = factor_of * one(*cut)
    return factor_of


def different_ones(rng, rows, count, top, lift):
    order = jax.random.permutation(jax.random.fold_in(rng, 1), count)
    pull = order
    for power in range(3):
        pull = pull * pull // count
    pull = pull * lift // count
    tickets = jax.random.randint(jax.random.fold_in(rng, 2), (rows, count), 0, 4096) + pull
    holders = jax.random.permutation(jax.random.fold_in(rng, 3), rows)[jnp.arange(count) % rows]
    tickets = jnp.where(jnp.arange(rows)[:, None] == holders[None, :], 1 << 14, tickets)
    priority = tickets * count + jnp.arange(count)
    return lax.top_k(priority.astype(jnp.int32), top)[1].astype(jnp.int32)


def gaussian(own_key, shape, spread, limit, split=(), kind=jnp.bfloat16):
    entries = spread * jax.random.normal(own_key, shape, jnp.float32)
    if split:
        entries = entries * level_of(own_key, shape, split, -0.22, 0.18)
    return jnp.clip(entries, -limit, limit).astype(kind)


def setup_inputs(seed: int = 0) -> dict:
    seeds = jax.random.split(jax.random.key(seed), 4)
    trajectory = gaussian(seeds[0], (TIME, UNITS), 1.0, 6.0, ((0, 16), (1, 8)), jnp.float32)
    block_values = gaussian(seeds[1], (NBLK, SEL, BLOCK, BLOCK), (UNITS * SEL // KB) ** -0.5, 0.046875, ((0, 8),), jnp.float32)
    block_index = different_ones(seeds[2], NBLK, KB, SEL, 0)
    return dict(trajectory=trajectory, block_values=block_values, block_index=block_index)


def sketch_of(trajectory, block_values, block_index):
    rows = trajectory.shape[0]
    columns = jnp.arange(KB, dtype=jnp.int32)
    onehot = (block_index[:, :, None] == columns[None, None, :]).astype(jnp.float32)

    def step(index, total):
        start = (index * BLOCK).astype(jnp.int32)
        cols = lax.dynamic_slice_in_dim(trajectory, start, BLOCK, 1)
        tiles = lax.dynamic_index_in_dim(block_values, index, 0, keepdims=False)
        picks = lax.dynamic_index_in_dim(onehot, index, 0, keepdims=False)
        prod = jnp.einsum('rk,skc->rsc', cols, tiles, precision=lax.Precision.HIGHEST)
        added = jnp.einsum('rsc,sj->rjc', prod, picks, precision=lax.Precision.HIGHEST)
        return total + added.reshape(rows, KB * BLOCK)
    start_total = jnp.zeros((rows, KB * BLOCK), jnp.float32)
    return lax.fori_loop(0, NBLK, step, start_total)

def reference(trajectory, block_values, block_index):
    sketch = sketch_of(trajectory, block_values, block_index)
    gram = jnp.dot(sketch.T, sketch, precision=lax.Precision.HIGHEST) / TIME
    lower = jnp.linalg.cholesky(gram)
    basis = jax.scipy.linalg.solve_triangular(lower, sketch.T, lower=True).T
    return (basis, lower.T)
```

```python
import functools
import jax
import jax.numpy as jnp
from jax import lax
from jax.experimental import pallas as pl
from jax.experimental.pallas import tpu as pltpu
from jax.sharding import PartitionSpec as P

B = 128
N = 512
f32 = jnp.float32
bf16 = jnp.bfloat16


def split(x):
    hi = x.astype(bf16)
    return hi, (x - hi.astype(f32)).astype(bf16)


def dot3(a, b, dims):
    ah, al = split(a)
    bh, bl = split(b)
    dg = functools.partial(lax.dot_general, dimension_numbers=(dims, ((), ())), preferred_element_type=f32)
    return dg(ah, bh) + (dg(ah, bl) + dg(al, bh))


def row_of(x, p):
    return jnp.broadcast_to(x[p:p + 1, :], x.shape)


def lane_of(x, j):
    return jnp.broadcast_to(x[:, j:j + 1], x.shape)


def recip(x):
    return 1.0 / x


def factor_block(d):
    row = lax.broadcasted_iota(jnp.int32, (8, B), 0)
    lane = lax.broadcasted_iota(jnp.int32, (8, B), 1)
    us, ws = [], []
    for s in range(16):
        lo = 8 * s
        inside = (lane >= lo) & (lane < lo + 8)
        pre = d[s]
        cols = [lane_of(pre, lo + j) for j in range(8)]
        below = [[lane_of(d[t], lo + j) for j in range(8)] for t in range(s + 1, 16)]
        x1 = jnp.where(inside, (lane - lo == row).astype(f32), pre)
        x2 = jnp.where(inside, pre, 0.0)
        snap1 = snap2 = None
        piv = None
        for p in range(0, 8, 2):
            q = p + 1
            cp, cq = cols[p], cols[q]
            a, b, c = row_of(cp, p), row_of(cp, q), row_of(cq, q)
            det = a * c - b * b
            r = recip(det)
            ra = recip(a)
            isp, isq = row == p, row == q
            either = isp | isq
            mp = jnp.where(either, jnp.where(isp, -1.0, 0.0), cp)
            mq = jnp.where(either, jnp.where(isq, -1.0, 0.0), cq)

            def step(x, snap=None, want=False):
                xp, xq = row_of(x, p), row_of(x, q)
                yp = (c * xp - b * xq) * r
                yq = (a * xq - b * xp) * r
                new = jnp.where(either, 0.0, x) - (mp * yp + mq * yq)
                if not want:
                    return new
                second = xq - (b * ra) * xp
                snap = jnp.where(isp, xp, jnp.where(isq, second, 0.0 if snap is None else snap))
                return new, snap

            for j in range(p + 2, 8):
                cols[j] = step(cols[j])
            x1, snap1 = step(x1, snap1, True)
            x2, snap2 = step(x2, snap2, True)
            dd = jnp.where(isp, a, det * ra)
            piv = dd if piv is None else jnp.where(row >= p, dd, piv)
        scale = lax.rsqrt(piv)
        snap1 = snap1 * scale
        snap2 = snap2 * scale
        upper = jnp.where(inside & (lane - lo >= row), snap2, jnp.where(lane >= lo + 8, snap1, 0.0))
        us.append(upper)
        ws.append(jnp.where(lane < lo + 8, snap1, 0.0))
        v = [row_of(x1, j) for j in range(8)]
        new = list(d)
        for k, t in enumerate(range(s + 1, 16)):
            cb = below[k]
            upd = [cb[j] * v[j] for j in range(8)]
            while len(upd) > 1:
                upd = [upd[i] + upd[i + 1] for i in range(0, len(upd), 2)]
            new[t] = jnp.where(inside, 0.0, d[t]) - upd[0]
        d = new
    return us, ws


def finish_kernel(gram_ref, s_hbm, basis_hbm, factor_ref, a_ref, w_ref, s_ref, o_ref, sem, osem):
    rows = s_ref.shape[0]
    load = pltpu.make_async_copy(s_hbm, s_ref, sem)
    load.start()
    eye = (lax.broadcasted_iota(jnp.int32, (B, B), 0) == lax.broadcasted_iota(jnp.int32, (B, B), 1))
    dl, ds_ = [], []
    for b in range(4):
        blk = jnp.where(eye, gram_ref[b * B:(b + 1) * B, b * B:(b + 1) * B], 0.0)
        dl.append(jnp.sum(blk, axis=0, keepdims=True))
        ds_.append(jnp.sum(blk, axis=1, keepdims=True))
    diag_l = jnp.concatenate(dl, axis=1)
    rs_l = lax.rsqrt(diag_l)
    sq_l = diag_l * rs_l
    for b in range(4):
        a_ref[b * B:(b + 1) * B, :] = gram_ref[b * B:(b + 1) * B, :] * lax.rsqrt(ds_[b]) * rs_l
    factor_ref[...] = jnp.zeros_like(factor_ref)

    for b in range(4):
        lo = b * B
        d = [a_ref[lo + 8 * i:lo + 8 * i + 8, lo:lo + B] for i in range(16)]
        us, ws = factor_block(d)
        for i in range(16):
            factor_ref[lo + 8 * i:lo + 8 * i + 8, lo:lo + B] = us[i] * sq_l[:, lo:lo + B]
            w_ref[lo + 8 * i:lo + 8 * i + 8, lo:lo + B] = ws[i]
        w = jnp.concatenate(ws, axis=0)
        panel = a_ref[lo:lo + B, :]
        pp = dot3(w, panel, ((1,), (0,)))
        if b > 0:
            w_ref[lo:lo + B, :lo] = pp[:, :lo]
        if b < 3:
            factor_ref[lo:lo + B, lo + B:] = pp[:, lo + B:] * sq_l[:, lo + B:]
            w_ref[lo:lo + B, lo + B:] = jnp.zeros((B, N - lo - B), f32)
            full = jnp.concatenate([pp[:, :lo], w, pp[:, lo + B:]], axis=1) if b > 0 else jnp.concatenate([w, pp[:, lo + B:]], axis=1)
            upd = dot3(pp[:, lo + B:], full, ((0,), (0,)))
            a_ref[lo + B:, lo:lo + B] = jnp.zeros((N - lo - B, B), f32)
            a_ref[lo + B:, :] = a_ref[lo + B:, :] - upd
    wh, wl = split(w_ref[...] * rs_l)
    dg = functools.partial(lax.dot_general, dimension_numbers=(((1,), (1,)), ((), ())), preferred_element_type=f32)
    load.wait()
    outs = []
    step = 256
    for i in range(rows // step):
        sl = slice(i * step, (i + 1) * step)
        sh, slo = split(s_ref[sl, :])
        for h in range(2):
            k = 256 * (h + 1)
            c = slice(256 * h, k)
            o_ref[sl, c] = dg(sh[:, :k], wh[c, :k]) + (dg(sh[:, :k], wl[c, :k]) + dg(slo[:, :k], wh[c, :k]))
        cp = pltpu.make_async_copy(o_ref.at[sl, :], basis_hbm.at[sl, :], osem.at[i])
        cp.start()
        outs.append(cp)
    for cp in outs:
        cp.wait()


def finish(gram, sketch):
    rows = sketch.shape[0]
    return pl.pallas_call(
        finish_kernel,
        out_shape=(jax.ShapeDtypeStruct((rows, N), f32), jax.ShapeDtypeStruct((N, N), f32)),
        in_specs=[pl.BlockSpec(memory_space=pltpu.VMEM), pl.BlockSpec(memory_space=pl.ANY)],
        out_specs=(pl.BlockSpec(memory_space=pl.ANY), pl.BlockSpec(memory_space=pltpu.VMEM)),
        scratch_shapes=[
            pltpu.VMEM((N, N), f32), pltpu.VMEM((N, N), f32), pltpu.VMEM((rows, N), f32), pltpu.VMEM((rows, N), f32),
            pltpu.SemaphoreType.DMA(()), pltpu.SemaphoreType.DMA((rows // 256,)),
        ],
        compiler_params=pltpu.CompilerParams(vmem_limit_bytes=40 * 2**20),
        name="finish",
    )(gram, sketch)


BLOCK = 128
KB = 4


def from_behind(value, axis, steps):
    count = lax.axis_size(axis)
    pairs = [(source, (source + steps) % count) for source in range(count)]
    return lax.ppermute(value, axis, pairs)


def shards(trajectory, block_values, block_index):
    cycle_size = lax.axis_size("units")
    rows = trajectory.shape[0]
    share = rows // cycle_size
    local_units = trajectory.shape[1]
    nblocks = local_units // BLOCK
    columns = jnp.arange(KB, dtype=jnp.int32)
    onehot = (block_index[:, :, None] == columns[None, None, :]).astype(jnp.float32)

    def partial_rows(start, count):
        slab = lax.dynamic_slice_in_dim(trajectory, start, count, 0)
        slab = slab.reshape(count, nblocks, BLOCK)
        prod = jnp.einsum("rbk,bskc->rbsc", slab, block_values, precision=lax.Precision.HIGHEST)
        added = jnp.einsum("rbsc,bsj->rjc", prod, onehot, precision=lax.Precision.HIGHEST)
        return added.reshape(count, KB * BLOCK)

    place = lax.axis_index("units")
    first = jnp.mod(place - 1, cycle_size)
    total = partial_rows(first * share, share)
    for step in range(1, cycle_size):
        total = from_behind(total, "units", 1)
        target = jnp.mod(place - 1 - step, cycle_size)
        total = total + partial_rows(target * share, share)
    all_time = rows * lax.axis_size("tm")
    local_gram = jnp.dot(total.T, total, precision=lax.Precision.HIGHEST) / all_time
    gram = lax.psum(local_gram, ("tm", "units"))
    sketch = lax.all_gather(total, "units", axis=0, tiled=True)
    return finish(gram, sketch)


def solution(mesh):
    return jax.shard_map(
        shards,
        mesh=mesh,
        in_specs=(P("tm", "units"), P("units", None, None, None), P("units", None)),
        out_specs=(P("tm", None), P()),
        check_vma=False,
    )
```

```python
import functools
import jax
import jax.numpy as jnp
from jax import lax
from jax.experimental import pallas as pl
from jax.experimental.pallas import tpu as pltpu
from jax.sharding import PartitionSpec as P

B = 128
N = 512
f32 = jnp.float32
bf16 = jnp.bfloat16
MESH = pl.DeviceIdType.MESH
TILES = [(i, j) for i in range(4) for j in range(i, 4)]


def split(x):
    hi = x.astype(bf16)
    return hi, (x - hi.astype(f32)).astype(bf16)


def dot3(a, b, dims):
    ah, al = split(a)
    bh, bl = split(b)
    dg = functools.partial(lax.dot_general, dimension_numbers=(dims, ((), ())), preferred_element_type=f32)
    return dg(ah, bh) + (dg(ah, bl) + dg(al, bh))


def row_of(x, p):
    return jnp.broadcast_to(x[p:p + 1, :], x.shape)


def lane_of(x, j):
    return jnp.broadcast_to(x[:, j:j + 1], x.shape)


def recip(x):
    return 1.0 / x


def factor_block(d):
    row = lax.broadcasted_iota(jnp.int32, (8, B), 0)
    lane = lax.broadcasted_iota(jnp.int32, (8, B), 1)
    us, ws = [], []
    for s in range(16):
        lo = 8 * s
        inside = (lane >= lo) & (lane < lo + 8)
        pre = d[s]
        cols = [lane_of(pre, lo + j) for j in range(8)]
        below = [[lane_of(d[t], lo + j) for j in range(8)] for t in range(s + 1, 16)]
        x1 = jnp.where(inside, (lane - lo == row).astype(f32), pre)
        x2 = jnp.where(inside, pre, 0.0)
        snap1 = snap2 = None
        piv = None
        for p in range(0, 8, 2):
            q = p + 1
            cp, cq = cols[p], cols[q]
            a, b, c = row_of(cp, p), row_of(cp, q), row_of(cq, q)
            det = a * c - b * b
            r = recip(det)
            ra = recip(a)
            isp, isq = row == p, row == q
            either = isp | isq
            mp = jnp.where(either, jnp.where(isp, -1.0, 0.0), cp)
            mq = jnp.where(either, jnp.where(isq, -1.0, 0.0), cq)

            def step(x, snap=None, want=False):
                xp, xq = row_of(x, p), row_of(x, q)
                yp = (c * xp - b * xq) * r
                yq = (a * xq - b * xp) * r
                new = jnp.where(either, 0.0, x) - (mp * yp + mq * yq)
                if not want:
                    return new
                second = xq - (b * ra) * xp
                snap = jnp.where(isp, xp, jnp.where(isq, second, 0.0 if snap is None else snap))
                return new, snap

            for j in range(p + 2, 8):
                cols[j] = step(cols[j])
            x1, snap1 = step(x1, snap1, True)
            x2, snap2 = step(x2, snap2, True)
            dd = jnp.where(isp, a, det * ra)
            piv = dd if piv is None else jnp.where(row >= p, dd, piv)
        scale = lax.rsqrt(piv)
        snap1 = snap1 * scale
        snap2 = snap2 * scale
        upper = jnp.where(inside & (lane - lo >= row), snap2, jnp.where(lane >= lo + 8, snap1, 0.0))
        us.append(upper)
        ws.append(jnp.where(lane < lo + 8, snap1, 0.0))
        v = [row_of(x1, j) for j in range(8)]
        new = list(d)
        for k, t in enumerate(range(s + 1, 16)):
            cb = below[k]
            upd = [cb[j] * v[j] for j in range(8)]
            while len(upd) > 1:
                upd = [upd[i] + upd[i + 1] for i in range(0, len(upd), 2)]
            new[t] = jnp.where(inside, 0.0, d[t]) - upd[0]
        d = new
    return us, ws


def finish_kernel(gram_ref, s_hbm, basis_hbm, factor_ref, a_ref, w_ref, s_ref, o_ref, sem, osem):
    rows = s_ref.shape[0]
    load = pltpu.make_async_copy(s_hbm, s_ref, sem)
    load.start()
    eye = (lax.broadcasted_iota(jnp.int32, (B, B), 0) == lax.broadcasted_iota(jnp.int32, (B, B), 1))
    dl, ds_ = [], []
    tile_rows = {tile: slice(n * B, (n + 1) * B) for n, tile in enumerate(TILES)}
    for b in range(4):
        blk = jnp.where(eye, gram_ref[tile_rows[b, b], :], 0.0)
        dl.append(jnp.sum(blk, axis=0, keepdims=True))
        ds_.append(jnp.sum(blk, axis=1, keepdims=True))
    diag_l = jnp.concatenate(dl, axis=1)
    rs_l = lax.rsqrt(diag_l)
    sq_l = diag_l * rs_l
    for i, j in TILES:
        cols = slice(j * B, (j + 1) * B)
        a_ref[i * B:(i + 1) * B, cols] = gram_ref[tile_rows[i, j], :] * lax.rsqrt(ds_[i]) * rs_l[:, cols]
    for i in range(1, 4):
        a_ref[i * B:(i + 1) * B, :i * B] = jnp.zeros((B, i * B), f32)
    factor_ref[...] = jnp.zeros_like(factor_ref)

    for b in range(4):
        lo = b * B
        d = [a_ref[lo + 8 * i:lo + 8 * i + 8, lo:lo + B] for i in range(16)]
        us, ws = factor_block(d)
        for i in range(16):
            factor_ref[lo + 8 * i:lo + 8 * i + 8, lo:lo + B] = us[i] * sq_l[:, lo:lo + B]
            w_ref[lo + 8 * i:lo + 8 * i + 8, lo:lo + B] = ws[i]
        w = jnp.concatenate(ws, axis=0)
        panel = a_ref[lo:lo + B, :]
        pp = dot3(w, panel, ((1,), (0,)))
        if b > 0:
            w_ref[lo:lo + B, :lo] = pp[:, :lo]
        if b < 3:
            factor_ref[lo:lo + B, lo + B:] = pp[:, lo + B:] * sq_l[:, lo + B:]
            w_ref[lo:lo + B, lo + B:] = jnp.zeros((B, N - lo - B), f32)
            full = jnp.concatenate([pp[:, :lo], w, pp[:, lo + B:]], axis=1) if b > 0 else jnp.concatenate([w, pp[:, lo + B:]], axis=1)
            upd = dot3(pp[:, lo + B:], full, ((0,), (0,)))
            a_ref[lo + B:, lo:lo + B] = jnp.zeros((N - lo - B, B), f32)
            a_ref[lo + B:, :] = a_ref[lo + B:, :] - upd
    wh, wl = split(w_ref[...] * rs_l)
    dg = functools.partial(lax.dot_general, dimension_numbers=(((1,), (1,)), ((), ())), preferred_element_type=f32)
    load.wait()
    outs = []
    step = 256
    for i in range(rows // step):
        sl = slice(i * step, (i + 1) * step)
        sh, slo = split(s_ref[sl, :])
        for h in range(2):
            k = 256 * (h + 1)
            c = slice(256 * h, k)
            o_ref[sl, c] = dg(sh[:, :k], wh[c, :k]) + (dg(sh[:, :k], wl[c, :k]) + dg(slo[:, :k], wh[c, :k]))
        cp = pltpu.make_async_copy(o_ref.at[sl, :], basis_hbm.at[sl, :], osem.at[i])
        cp.start()
        outs.append(cp)
    for cp in outs:
        cp.wait()


def finish(gram, sketch):
    rows = sketch.shape[0]
    return pl.pallas_call(
        finish_kernel,
        out_shape=(jax.ShapeDtypeStruct((rows, N), f32), jax.ShapeDtypeStruct((N, N), f32)),
        in_specs=[pl.BlockSpec(memory_space=pltpu.VMEM), pl.BlockSpec(memory_space=pl.ANY)],
        out_specs=(pl.BlockSpec(memory_space=pl.ANY), pl.BlockSpec(memory_space=pltpu.VMEM)),
        scratch_shapes=[
            pltpu.VMEM((N, N), f32), pltpu.VMEM((N, N), f32), pltpu.VMEM((rows, N), f32), pltpu.VMEM((rows, N), f32),
            pltpu.SemaphoreType.DMA(()), pltpu.SemaphoreType.DMA((rows // 256,)),
        ],
        compiler_params=pltpu.CompilerParams(vmem_limit_bytes=40 * 2**20),
        name="finish",
    )(gram, sketch)


def positions():
    tm, u = lax.axis_index("tm"), lax.axis_index("units")
    return tm // 4, lax.rem(tm, 4), u // 2, lax.rem(u, 2)


def device(y, x, z, c):
    return (lax.rem(y, 4) * 4 + lax.rem(x, 4), lax.rem(z, 4) * 2 + lax.rem(c, 2))


def sketch_kernel(all_time, index_ref, x_hbm, values_hbm, sketch_hbm, gram_ref,
                  xbuf, values, wh, wl, part, from_core, far, far_in, near, near_in, share,
                  grams, gram_core, plane, piece, pieces,
                  xsem, vsem, core_s, core_r, far_s, far_r, near_s, near_r, g1_s, g1_r, g2_s, g2_r, g3_s, g3_r,
                  g4_s, g4_r, g5_s, g5_r, sk_s, sk_r, fw_s, fw_r, own_sem):
    y, x, z, c = positions()
    me = y * 4 + x
    sibling = device(y, x, z, c + 1)
    up, down, across = device(y, x, z + 1, c), device(y, x, z + 3, c), device(y, x, z + 2, c)

    def remote(src, dst, ssem, rsem, to):
        return pltpu.make_async_remote_copy(src_ref=src, dst_ref=dst, send_sem=ssem, recv_sem=rsem,
                                            device_id=to, device_id_type=MESH)

    barrier = pltpu.get_barrier_semaphore()
    for to in (sibling, up, down, across):
        pl.semaphore_signal(barrier, inc=1, device_id=to, device_id_type=MESH)

    def greet(i, carry):
        other = lax.rem(me + i, 16)
        pl.semaphore_signal(barrier, inc=1, device_id=device(other // 4, lax.rem(other, 4), z, c), device_id_type=MESH)
        return carry

    lax.fori_loop(1, 16, greet, 0)

    vload = pltpu.make_async_copy(values_hbm, values, vsem)
    vload.start()
    order = [lax.rem(z + 2, 4), lax.rem(z + 1, 4), lax.rem(z + 3, 4), z]
    xloads = []
    for t in range(4):
        cp = pltpu.make_async_copy(x_hbm.at[pl.ds(order[t] * 256, 256), :], xbuf.at[t], xsem.at[t])
        cp.start()
        xloads.append(cp)
    vload.wait()

    def place(b, carry):
        first, second = index_ref[b, 0], index_ref[b, 1]
        t0, t1 = values[b, 0], values[b, 1]
        rows = pl.ds(pl.multiple_of(b * B, B), B)
        for j in range(4):
            tile = jnp.where(first == j, t0, jnp.where(second == j, t1, 0.0))
            hi, lo = split(tile)
            wh[rows, j * B:(j + 1) * B] = hi
            wl[rows, j * B:(j + 1) * B] = lo
        return carry

    lax.fori_loop(0, values.shape[0], place, 0)
    kc = 512
    nk = xbuf.shape[2] // kc

    def product(t, begin, end):
        def body(k, carry):
            cols = pl.ds(pl.multiple_of(k * kc, kc), kc)
            xh, xl = split(xbuf[t, :, cols])
            h, l = wh[cols, :], wl[cols, :]
            dot = functools.partial(jnp.dot, preferred_element_type=f32)
            r = dot(xh, h) + (dot(xh, l) + dot(xl, h))
            if begin == 0:
                prev = jnp.where(k == 0, 0.0, part[t])
            else:
                prev = part[t]
            part[t] = prev + r
            return carry
        lax.fori_loop(begin, end, body, 0)

    mine = pl.ds(pl.multiple_of(c * B, B), B)
    theirs = pl.ds(pl.multiple_of((1 - c) * B, B), B)
    core_cps = [remote(part.at[t, theirs, :], from_core.at[t], core_s.at[t], core_r.at[t], sibling) for t in range(4)]
    far_up = remote(far.at[0:64], far_in.at[0], far_s.at[0], far_r.at[0], up)
    far_down = remote(far.at[64:128], far_in.at[1], far_s.at[1], far_r.at[1], down)
    near_up = remote(near.at[0], near_in.at[0], near_s.at[0], near_r.at[0], up)
    near_down = remote(near.at[1], near_in.at[1], near_s.at[1], near_r.at[1], down)

    def both(t):
        core_cps[t].wait_recv()
        return part[t, mine, :] + from_core[t]

    for t in range(4):
        xloads[t].wait()
        if t == 0:
            part[0] = jnp.zeros_like(part[0])
        product(t, 0, nk // 2)
        if t == 1:
            far[...] = both(0)
            far_up.start()
            far_down.start()
        if t == 2:
            s = both(1)
            far_up.wait_recv()
            near[0, 64:128, :] = s[64:128]
            near[0, 0:64, :] = s[0:64] + far_in[0]
            near_up.start()
        if t == 3:
            s = both(2)
            far_down.wait_recv()
            near[1, 0:64, :] = s[0:64]
            near[1, 64:128, :] = s[64:128] + far_in[1]
            near_down.start()
        product(t, nk // 2, nk)
        if t == 0:
            pl.semaphore_wait(barrier, 19)
        core_cps[t].start()
    own = both(3)
    near_up.wait_recv()
    own = own + near_in[0]
    near_down.wait_recv()
    own = own + near_in[1]
    share[...] = own

    row0 = pl.multiple_of((z * 2 + c) * B, B)
    dest = sketch_hbm.at[pl.ds(row0, B), :]
    sk = [remote(share, dest, sk_s.at[i], sk_r.at[i], to) for i, to in enumerate((up, down, across))]

    sh, sl = split(own)
    tdot = functools.partial(lax.dot_general, dimension_numbers=(((0,), (0,)), ((), ())), preferred_element_type=f32)
    n = 0
    for i in range(4):
        a = slice(i * B, (i + 1) * B)
        r = tdot(sh[:, a], sh[:, i * B:]) + (tdot(sh[:, a], sl[:, i * B:]) + tdot(sl[:, a], sh[:, i * B:]))
        for j in range(4 - i):
            grams[n * B:(n + 1) * B, :] = r[:, j * B:(j + 1) * B]
            n += 1
    half = 5 * B
    my_half = pl.ds(pl.multiple_of(c * half, half), half)
    their_half = pl.ds(pl.multiple_of((1 - c) * half, half), half)
    g1 = remote(grams.at[their_half, :], gram_core, g1_s, g1_r, sibling)
    g1.start()
    for cp in sk:
        cp.start()
    own_store = pltpu.make_async_copy(share, dest, own_sem)
    own_store.start()
    forward = [remote(share, dest, fw_s.at[0], fw_r.at[0], sibling)]
    forward[0].start()
    g1.wait_recv()
    gram_core[...] = gram_core[...] + grams[my_half, :]

    rows = half // 16

    def span(k):
        return pl.ds(pl.multiple_of(k * rows, 8), rows)

    def scatter(i):
        k = lax.rem(me + i, 16)
        return remote(gram_core.at[span(k), :], plane.at[me], g2_s.at[i], g2_r.at[i], device(k // 4, lax.rem(k, 4), z, c))

    for i in range(1, 16):
        scatter(i).start()
    plane[me] = gram_core[span(me), :]
    for i in range(1, 16):
        scatter(i).wait_recv()
    total = plane[0]
    for k in range(1, 16):
        total = total + plane[k]
    piece[...] = total
    pieces[z] = total
    g3 = [remote(piece, pieces.at[z], g3_s.at[i], g3_r.at[i], to) for i, to in enumerate((up, down, across))]
    for cp in g3:
        cp.start()
    for cp in g3:
        cp.wait_recv()
    total = ((pieces[0] + pieces[1]) + (pieces[2] + pieces[3])) / all_time
    my_rows = pl.ds(pl.multiple_of(c * half + me * rows, 8), rows)
    gram_ref[my_rows, :] = total

    def gather(i):
        k = lax.rem(me + i, 16)
        return remote(gram_ref.at[my_rows, :], gram_ref.at[my_rows, :], g4_s.at[i], g4_r.at[i], device(k // 4, lax.rem(k, 4), z, c))

    for i in range(1, 16):
        gather(i).start()
    for i, steps in ((0, 3), (1, 1), (2, 2)):
        sk[i].wait_recv()
        came = pl.multiple_of((lax.rem(z + steps, 4) * 2 + c) * B, B)
        block = sketch_hbm.at[pl.ds(came, B), :]
        cp = remote(block, block, fw_s.at[1 + i], fw_r.at[1 + i], sibling)
        cp.start()
        forward.append(cp)
    for i in range(1, 16):
        gather(i).wait_recv()
    g5 = remote(gram_ref.at[my_half, :], gram_ref.at[my_half, :], g5_s, g5_r, sibling)
    g5.start()
    for cp in core_cps:
        cp.wait_send()
    for cp in (far_up, far_down, near_up, near_down, g1, *g3, *sk):
        cp.wait_send()
    for i in range(1, 16):
        scatter(i).wait_send()
        gather(i).wait_send()
    own_store.wait()
    for cp in forward:
        cp.wait()
    g5.wait()


def sketch_and_gram(all_time, index, trajectory, values):
    rows, units = trajectory.shape
    dma = pltpu.SemaphoreType.DMA
    return pl.pallas_call(
        functools.partial(sketch_kernel, all_time),
        out_shape=(jax.ShapeDtypeStruct((rows, N), f32), jax.ShapeDtypeStruct((10 * B, B), f32)),
        in_specs=[pl.BlockSpec(memory_space=pltpu.SMEM), pl.BlockSpec(memory_space=pl.ANY), pl.BlockSpec(memory_space=pl.ANY)],
        out_specs=(pl.BlockSpec(memory_space=pl.ANY), pl.BlockSpec(memory_space=pltpu.VMEM)),
        scratch_shapes=[
            pltpu.VMEM((4, rows // 4, units), f32), pltpu.VMEM(values.shape, f32),
            pltpu.VMEM((units, N), bf16), pltpu.VMEM((units, N), bf16),
            pltpu.VMEM((4, rows // 4, N), f32), pltpu.VMEM((4, B, N), f32),
            pltpu.VMEM((B, N), f32), pltpu.VMEM((2, B // 2, N), f32),
            pltpu.VMEM((2, B, N), f32), pltpu.VMEM((2, B, N), f32), pltpu.VMEM((B, N), f32),
            pltpu.VMEM((10 * B, B), f32), pltpu.VMEM((5 * B, B), f32), pltpu.VMEM((16, 40, B), f32),
            pltpu.VMEM((40, B), f32), pltpu.VMEM((4, 40, B), f32),
            dma((4,)), dma(()), dma((4,)), dma((4,)), dma((2,)), dma((2,)), dma((2,)), dma((2,)), dma(()), dma(()),
            dma((16,)), dma((16,)), dma((3,)), dma((3,)), dma((16,)), dma((16,)), dma(()), dma(()),
            dma((3,)), dma((3,)), dma((4,)), dma((4,)), dma(()),
        ],
        compiler_params=pltpu.CompilerParams(collective_id=0, has_side_effects=True, vmem_limit_bytes=52 * 2**20),
        name="sketch_and_gram",
    )(index, trajectory, values)


def shards(trajectory, block_values, block_index):
    all_time = trajectory.shape[0] * lax.axis_size("tm")
    sketch, gram = sketch_and_gram(all_time, block_index, trajectory, block_values)
    return finish(gram, sketch)


def solution(mesh):
    return jax.shard_map(
        shards,
        mesh=mesh,
        in_specs=(P("tm", "units"), P("units", None, None, None), P("units", None)),
        out_specs=(P("tm", None), P()),
        check_vma=False,
    )
```

```python
import functools
import jax
import jax.numpy as jnp
from jax import lax
from jax.experimental import pallas as pl
from jax.experimental.pallas import tpu as pltpu
from jax.sharding import PartitionSpec as P

B = 128
N = 512
f32 = jnp.float32
bf16 = jnp.bfloat16
MESH = pl.DeviceIdType.MESH
TILES = [(i, j) for i in range(4) for j in range(i, 4)]


def split(x):
    hi = x.astype(bf16)
    return hi, (x - hi.astype(f32)).astype(bf16)


def dot3(a, b, dims):
    ah, al = split(a)
    bh, bl = split(b)
    dg = functools.partial(lax.dot_general, dimension_numbers=(dims, ((), ())), preferred_element_type=f32)
    return dg(ah, bh) + (dg(ah, bl) + dg(al, bh))


def row_of(x, p):
    return jnp.broadcast_to(x[p:p + 1, :], x.shape)


def lane_of(x, j):
    return jnp.broadcast_to(x[:, j:j + 1], x.shape)


def recip(x):
    return 1.0 / x


def factor_block(d):
    row = lax.broadcasted_iota(jnp.int32, (8, B), 0)
    lane = lax.broadcasted_iota(jnp.int32, (8, B), 1)
    us, ws = [], []
    for s in range(16):
        lo = 8 * s
        inside = (lane >= lo) & (lane < lo + 8)
        pre = d[s]
        cols = [lane_of(pre, lo + j) for j in range(8)]
        below = [[lane_of(d[t], lo + j) for j in range(8)] for t in range(s + 1, 16)]
        x1 = jnp.where(inside, (lane - lo == row).astype(f32), pre)
        x2 = jnp.where(inside, pre, 0.0)
        snap1 = snap2 = None
        piv = None
        for p in range(0, 8, 2):
            q = p + 1
            cp, cq = cols[p], cols[q]
            a, b, c = row_of(cp, p), row_of(cp, q), row_of(cq, q)
            det = a * c - b * b
            r = recip(det)
            ra = recip(a)
            isp, isq = row == p, row == q
            either = isp | isq
            mp = jnp.where(either, jnp.where(isp, -1.0, 0.0), cp)
            mq = jnp.where(either, jnp.where(isq, -1.0, 0.0), cq)

            def step(x, snap=None, want=False):
                xp, xq = row_of(x, p), row_of(x, q)
                yp = (c * xp - b * xq) * r
                yq = (a * xq - b * xp) * r
                new = jnp.where(either, 0.0, x) - (mp * yp + mq * yq)
                if not want:
                    return new
                second = xq - (b * ra) * xp
                snap = jnp.where(isp, xp, jnp.where(isq, second, 0.0 if snap is None else snap))
                return new, snap

            for j in range(p + 2, 8):
                cols[j] = step(cols[j])
            x1, snap1 = step(x1, snap1, True)
            x2, snap2 = step(x2, snap2, True)
            dd = jnp.where(isp, a, det * ra)
            piv = dd if piv is None else jnp.where(row >= p, dd, piv)
        scale = lax.rsqrt(piv)
        snap1 = snap1 * scale
        snap2 = snap2 * scale
        upper = jnp.where(inside & (lane - lo >= row), snap2, jnp.where(lane >= lo + 8, snap1, 0.0))
        us.append(upper)
        ws.append(jnp.where(lane < lo + 8, snap1, 0.0))
        v = [row_of(x1, j) for j in range(8)]
        new = list(d)
        for k, t in enumerate(range(s + 1, 16)):
            cb = below[k]
            upd = [cb[j] * v[j] for j in range(8)]
            while len(upd) > 1:
                upd = [upd[i] + upd[i + 1] for i in range(0, len(upd), 2)]
            new[t] = jnp.where(inside, 0.0, d[t]) - upd[0]
        d = new
    return us, ws


def finish_kernel(gram_ref, s_hbm, basis_hbm, factor_ref, a_ref, w_ref, s_ref, o_ref, sem, osem):
    rows = s_ref.shape[0]
    load = pltpu.make_async_copy(s_hbm, s_ref, sem)
    load.start()
    eye = (lax.broadcasted_iota(jnp.int32, (B, B), 0) == lax.broadcasted_iota(jnp.int32, (B, B), 1))
    dl, ds_ = [], []
    tile_rows = {tile: slice(n * B, (n + 1) * B) for n, tile in enumerate(TILES)}
    for b in range(4):
        blk = jnp.where(eye, gram_ref[tile_rows[b, b], :], 0.0)
        dl.append(jnp.sum(blk, axis=0, keepdims=True))
        ds_.append(jnp.sum(blk, axis=1, keepdims=True))
    diag_l = jnp.concatenate(dl, axis=1)
    rs_l = lax.rsqrt(diag_l)
    sq_l = diag_l * rs_l
    for i, j in TILES:
        cols = slice(j * B, (j + 1) * B)
        a_ref[i * B:(i + 1) * B, cols] = gram_ref[tile_rows[i, j], :] * lax.rsqrt(ds_[i]) * rs_l[:, cols]
    for i in range(1, 4):
        a_ref[i * B:(i + 1) * B, :i * B] = jnp.zeros((B, i * B), f32)
    factor_ref[...] = jnp.zeros_like(factor_ref)

    for b in range(4):
        lo = b * B
        d = [a_ref[lo + 8 * i:lo + 8 * i + 8, lo:lo + B] for i in range(16)]
        us, ws = factor_block(d)
        for i in range(16):
            factor_ref[lo + 8 * i:lo + 8 * i + 8, lo:lo + B] = us[i] * sq_l[:, lo:lo + B]
            w_ref[lo + 8 * i:lo + 8 * i + 8, lo:lo + B] = ws[i]
        w = jnp.concatenate(ws, axis=0)
        panel = a_ref[lo:lo + B, :]
        pp = dot3(w, panel, ((1,), (0,)))
        if b > 0:
            w_ref[lo:lo + B, :lo] = pp[:, :lo]
        if b < 3:
            factor_ref[lo:lo + B, lo + B:] = pp[:, lo + B:] * sq_l[:, lo + B:]
            w_ref[lo:lo + B, lo + B:] = jnp.zeros((B, N - lo - B), f32)
            full = jnp.concatenate([pp[:, :lo], w, pp[:, lo + B:]], axis=1) if b > 0 else jnp.concatenate([w, pp[:, lo + B:]], axis=1)
            upd = dot3(pp[:, lo + B:], full, ((0,), (0,)))
            a_ref[lo + B:, lo:lo + B] = jnp.zeros((N - lo - B, B), f32)
            a_ref[lo + B:, :] = a_ref[lo + B:, :] - upd
    wh, wl = split(w_ref[...] * rs_l)
    dg = functools.partial(lax.dot_general, dimension_numbers=(((1,), (1,)), ((), ())), preferred_element_type=f32)
    load.wait()
    outs = []
    step = 256
    for i in range(rows // step):
        sl = slice(i * step, (i + 1) * step)
        sh, slo = split(s_ref[sl, :])
        for h in range(2):
            k = 256 * (h + 1)
            c = slice(256 * h, k)
            o_ref[sl, c] = dg(sh[:, :k], wh[c, :k]) + (dg(sh[:, :k], wl[c, :k]) + dg(slo[:, :k], wh[c, :k]))
        cp = pltpu.make_async_copy(o_ref.at[sl, :], basis_hbm.at[sl, :], osem.at[i])
        cp.start()
        outs.append(cp)
    for cp in outs:
        cp.wait()


def finish(gram, sketch):
    rows = sketch.shape[0]
    return pl.pallas_call(
        finish_kernel,
        out_shape=(jax.ShapeDtypeStruct((rows, N), f32), jax.ShapeDtypeStruct((N, N), f32)),
        in_specs=[pl.BlockSpec(memory_space=pltpu.VMEM), pl.BlockSpec(memory_space=pl.ANY)],
        out_specs=(pl.BlockSpec(memory_space=pl.ANY), pl.BlockSpec(memory_space=pltpu.VMEM)),
        scratch_shapes=[
            pltpu.VMEM((N, N), f32), pltpu.VMEM((N, N), f32), pltpu.VMEM((rows, N), f32), pltpu.VMEM((rows, N), f32),
            pltpu.SemaphoreType.DMA(()), pltpu.SemaphoreType.DMA((rows // 256,)),
        ],
        compiler_params=pltpu.CompilerParams(vmem_limit_bytes=64 * 2**20),
        name="finish",
    )(gram, sketch)


def positions():
    tm, u = lax.axis_index("tm"), lax.axis_index("units")
    return tm // 4, lax.rem(tm, 4), u // 2, lax.rem(u, 2)


def device(y, x, z, c):
    return (lax.rem(y, 4) * 4 + lax.rem(x, 4), lax.rem(z, 4) * 2 + lax.rem(c, 2))


PLANE = sorted(((dy, dx) for dy in range(4) for dx in range(4) if dy or dx),
               key=lambda o: -(min(o[0], 4 - o[0]) + min(o[1], 4 - o[1])))


def sketch_kernel(all_time, index_ref, x_hbm, values_hbm, sketch_hbm, gram_ref,
                  xbuf, values, wh, wl, part, from_core, far, far_in, near, near_in, share,
                  gram_core, plane, piece, pieces,
                  xsem, vsem, core_s, core_r, far_s, far_r, near_s, near_r, g2_s, g2_r, g3_s, g3_r,
                  g4_s, g4_r, g5_s, g5_r, sk_s, sk_r, fw_s, fw_r, own_sem):
    y, x, z, c = positions()
    me = y * 4 + x
    sibling = device(y, x, z, c + 1)
    up, down, across = device(y, x, z + 1, c), device(y, x, z + 3, c), device(y, x, z + 2, c)

    def remote(src, dst, ssem, rsem, to):
        return pltpu.make_async_remote_copy(src_ref=src, dst_ref=dst, send_sem=ssem, recv_sem=rsem,
                                            device_id=to, device_id_type=MESH)

    def inside(to):
        pl.semaphore_signal(pltpu.get_barrier_semaphore(), inc=1, device_id=to, device_id_type=MESH)

    groups = 4
    per = values.shape[0] // groups
    vloads = [pltpu.make_async_copy(values_hbm.at[pl.ds(g * per, per)], values.at[pl.ds(g * per, per)], vsem.at[g])
              for g in range(groups)]
    half = B // 2
    xloads = [[] for _ in range(4)]

    def fetch(t, to, row, count, n):
        xloads[t].append(pltpu.make_async_copy(x_hbm.at[pl.ds(pl.multiple_of(row, half), count), :],
                                               xbuf.at[t, pl.ds(to, count), :], xsem.at[t, n]))

    fetch(0, 0, lax.rem(z + 2, 4) * 256, 256, 0)
    for t in (1, 2):
        for n in range(4):
            target = lax.rem(z + (1, 3)[n % 2], 4)
            fetch(t, n * half, target * 256 + (n // 2) * B + (t - 1) * half, half, n)
    fetch(3, 0, z * 256, 256, 0)
    vloads[0].start()
    xloads[0][0].start()
    for cp in vloads[1:]:
        cp.start()
    for t in range(1, 4):
        for cp in xloads[t]:
            cp.start()
    for to in (sibling, up, down, across):
        inside(to)
    for dy, dx in PLANE:
        inside(device(y + dy, x + dx, z, c))

    def product(t, k, begin=False):
        results = []
        for e in range(per):
            b = k * per + e
            rows = pl.ds(pl.multiple_of(b * B, B), B)
            if t == 0:
                h0, l0 = split(values[b, 0])
                h1, l1 = split(values[b, 1])
                high = jnp.concatenate([h0, h1], axis=1)
                low = jnp.concatenate([l0, l1], axis=1)
                wh[rows, :] = high
                wl[rows, :] = low
            else:
                high, low = wh[rows, :], wl[rows, :]
            xh, xl = split(xbuf[t, :, rows])
            dot = functools.partial(jnp.dot, preferred_element_type=f32)
            results.append(dot(jnp.concatenate([xh, xl], axis=1), jnp.concatenate([high, high], axis=0)) + dot(xh, low))
        for j in range(4):
            cols = slice(j * B, (j + 1) * B)
            total = 0.0 if begin else part[t, :, cols]
            for e in range(per):
                b = k * per + e
                total = total + jnp.where(index_ref[0, b] == j, results[e][:, :B],
                                          jnp.where(index_ref[1, b] == j, results[e][:, B:], 0.0))
            part[t, :, cols] = total

    def products(t, begin):
        def body(k, carry):
            product(t, k)
            return carry
        lax.fori_loop(begin, groups, body, 0)

    mine = pl.ds(pl.multiple_of(c * B, B), B)
    theirs = pl.ds(pl.multiple_of((1 - c) * B, B), B)
    core_cps = [remote(part.at[t, theirs, :], from_core.at[t], core_s.at[t], core_r.at[t], sibling) for t in range(4)]
    far_cps = [remote(far.at[pl.ds(d * half, half), :], far_in.at[d], far_s.at[d], far_r.at[d], (up, down)[d])
               for d in range(2)]
    near_cps = [[remote(near.at[h, d], near_in.at[h, d], near_s.at[h, d], near_r.at[h, d], (up, down)[d])
                 for d in range(2)] for h in range(2)]

    def both(t):
        core_cps[t].wait_recv()
        return part[t, mine, :] + from_core[t]

    for t in range(4):
        for cp in xloads[t]:
            cp.wait()
        if t == 0:
            for g in range(groups):
                vloads[g].wait()
                product(0, g, g == 0)
            pl.semaphore_wait(pltpu.get_barrier_semaphore(), 19)
        else:
            product(t, 0, True)
            s = both(t - 1)
            if t == 1:
                far[...] = s
                for cp in far_cps:
                    cp.start()
            else:
                h = t - 2
                far_cps[h].wait_recv()
                for d in range(2):
                    add = s[d * half:(d + 1) * half]
                    near[h, d] = add + far_in[h] if d == h else add
                    near_cps[h][d].start()
            products(t, 1)
        core_cps[t].start()
    own = both(3)
    for h in range(2):
        near_cps[h][0].wait_recv()
        near_cps[h][1].wait_recv()
        rows = slice(h * half, (h + 1) * half)
        share[pl.ds(pl.multiple_of(c * B + h * half, half), half), :] = own[rows] + near_in[h, 0] + near_in[h, 1]

    row0 = pl.multiple_of((z * 2 + c) * B, B)
    dest = sketch_hbm.at[pl.ds(row0, B), :]
    swap = remote(share.at[mine, :], share.at[mine, :], fw_s.at[0], fw_r.at[0], sibling)
    swap.start()
    sk = [remote(share.at[mine, :], dest, sk_s.at[i], sk_r.at[i], to) for i, to in enumerate((up, down, across))]
    for cp in sk:
        cp.start()
    swap.wait_recv()
    chip_rows = pl.ds(pl.multiple_of(z * 256, 256), 256)
    own_store = pltpu.make_async_copy(share, sketch_hbm.at[chip_rows, :], own_sem)
    own_store.start()

    tdot = functools.partial(lax.dot_general, dimension_numbers=(((0,), (0,)), ((), ())), preferred_element_type=f32)
    for n in range(5):
        (i0, j0), (i1, j1) = TILES[n], TILES[n + 5]
        i, j = jnp.where(c == 0, i0, i1), jnp.where(c == 0, j0, j1)
        ah, al = split(share[:, pl.ds(pl.multiple_of(i * B, B), B)])
        bh, bl = split(share[:, pl.ds(pl.multiple_of(j * B, B), B)])
        gram_core[n * B:(n + 1) * B, :] = tdot(ah, bh) + (tdot(ah, bl) + tdot(al, bh))

    core_half = 5 * B
    rows = core_half // 16

    def span(k):
        return pl.ds(pl.multiple_of(k * rows, 8), rows)

    scatters = []
    for n, (dy, dx) in enumerate(PLANE):
        to = device(y + dy, x + dx, z, c)
        scatters.append(remote(gram_core.at[span(to[0]), :], plane.at[me], g2_s.at[n], g2_r.at[n], to))
    for cp in scatters:
        cp.start()
    plane[me] = gram_core[span(me), :]
    for cp in scatters:
        cp.wait_recv()
    total = plane[0]
    for k in range(1, 16):
        total = total + plane[k]
    piece[...] = total
    pieces[z] = total
    g3 = [remote(piece, pieces.at[z], g3_s.at[i], g3_r.at[i], to) for i, to in enumerate((across, up, down))]
    for cp in g3:
        cp.start()
    for cp in g3:
        cp.wait_recv()
    total = ((pieces[0] + pieces[1]) + (pieces[2] + pieces[3])) / all_time
    my_half = pl.ds(pl.multiple_of(c * core_half, core_half), core_half)
    my_rows = gram_ref.at[pl.ds(pl.multiple_of(c * core_half + me * rows, 8), rows), :]
    gram_ref[pl.ds(pl.multiple_of(c * core_half + me * rows, 8), rows), :] = total
    gathers = [remote(my_rows, my_rows, g4_s.at[n], g4_r.at[n], device(y + dy, x + dx, z, c))
               for n, (dy, dx) in enumerate(PLANE)]
    for cp in gathers:
        cp.start()
    forward = []
    for i, steps in ((0, 3), (1, 1), (2, 2)):
        sk[i].wait_recv()
        came = pl.multiple_of((lax.rem(z + steps, 4) * 2 + c) * B, B)
        block = sketch_hbm.at[pl.ds(came, B), :]
        cp = remote(block, block, fw_s.at[1 + i], fw_r.at[1 + i], sibling)
        cp.start()
        forward.append(cp)
    for cp in gathers:
        cp.wait_recv()
    g5 = remote(gram_ref.at[my_half, :], gram_ref.at[my_half, :], g5_s, g5_r, sibling)
    g5.start()
    for cp in (*core_cps, *far_cps, *near_cps[0], *near_cps[1], *g3, *sk, *scatters, *gathers, swap):
        cp.wait_send()
    own_store.wait()
    for cp in forward:
        cp.wait()
    g5.wait()


def sketch_and_gram(all_time, index, trajectory, values):
    rows, units = trajectory.shape
    dma = pltpu.SemaphoreType.DMA
    half = B // 2
    return pl.pallas_call(
        functools.partial(sketch_kernel, all_time),
        out_shape=(jax.ShapeDtypeStruct((rows, N), f32), jax.ShapeDtypeStruct((10 * B, B), f32)),
        in_specs=[pl.BlockSpec(memory_space=pltpu.SMEM), pl.BlockSpec(memory_space=pl.ANY), pl.BlockSpec(memory_space=pl.ANY)],
        out_specs=(pl.BlockSpec(memory_space=pl.ANY), pl.BlockSpec(memory_space=pltpu.VMEM)),
        scratch_shapes=[
            pltpu.VMEM((4, rows // 4, units), f32), pltpu.VMEM(values.shape, f32),
            pltpu.VMEM((units, 2 * B), bf16), pltpu.VMEM((units, 2 * B), bf16),
            pltpu.VMEM((4, rows // 4, N), f32), pltpu.VMEM((4, B, N), f32),
            pltpu.VMEM((B, N), f32), pltpu.VMEM((2, half, N), f32),
            pltpu.VMEM((2, 2, half, N), f32), pltpu.VMEM((2, 2, half, N), f32), pltpu.VMEM((2 * B, N), f32),
            pltpu.VMEM((5 * B, B), f32), pltpu.VMEM((16, 40, B), f32),
            pltpu.VMEM((40, B), f32), pltpu.VMEM((4, 40, B), f32),
            dma((4, 4)), dma((4,)), dma((4,)), dma((4,)), dma((2,)), dma((2,)), dma((2, 2)), dma((2, 2)),
            dma((16,)), dma((16,)), dma((3,)), dma((3,)), dma((16,)), dma((16,)), dma(()), dma(()),
            dma((3,)), dma((3,)), dma((4,)), dma((4,)), dma(()),
        ],
        compiler_params=pltpu.CompilerParams(collective_id=0, has_side_effects=True, vmem_limit_bytes=64 * 2**20),
        name="sketch_and_gram",
    )(index, trajectory, values)


def shards(trajectory, block_values, block_index):
    all_time = trajectory.shape[0] * lax.axis_size("tm")
    sketch, gram = sketch_and_gram(all_time, block_index.T, trajectory, block_values)
    return finish(gram, sketch)


def solution(mesh):
    return jax.shard_map(
        shards,
        mesh=mesh,
        in_specs=(P("tm", "units"), P("units", None, None, None), P("units", None)),
        out_specs=(P("tm", None), P()),
        check_vma=False,
    )
```

```python
import functools
import jax
import jax.numpy as jnp
from jax import lax
from jax.experimental import pallas as pl
from jax.experimental.pallas import tpu as pltpu
from jax.sharding import PartitionSpec as P

B = 128
N = 512
f32 = jnp.float32
bf16 = jnp.bfloat16
MESH = pl.DeviceIdType.MESH
TILES = [(i, j) for i in range(4) for j in range(i, 4)]


def split(x):
    hi = x.astype(bf16)
    return hi, (x - hi.astype(f32)).astype(bf16)


def dot3(a, b, dims):
    ah, al = split(a)
    bh, bl = split(b)
    dg = functools.partial(lax.dot_general, dimension_numbers=(dims, ((), ())), preferred_element_type=f32)
    return dg(ah, bh) + (dg(ah, bl) + dg(al, bh))


def row_of(x, p):
    return jnp.broadcast_to(x[p:p + 1, :], x.shape)


def lane_of(x, j):
    return jnp.broadcast_to(x[:, j:j + 1], x.shape)


def recip(x):
    return 1.0 / x


def three(x):
    high = x.astype(bf16).astype(f32)
    mid = (x - high).astype(bf16).astype(f32)
    return high, mid, x - high - mid


def products_of(a, b):
    ah, am, al = three(a)
    bh, bm, bl = three(b)
    a = jnp.concatenate([ah, ah, am, ah, al, am], axis=0).astype(bf16)
    b = jnp.concatenate([bh, bm, bh, bl, bh, bm], axis=0).astype(bf16)
    return lax.dot_general(a, b, (((0,), (0,)), ((), ())), preferred_element_type=f32)


def tree(terms):
    while len(terms) > 1:
        terms = [terms[i] + terms[i + 1] for i in range(0, len(terms), 2)]
    return terms[0]


def factor_block(d):
    row = lax.broadcasted_iota(jnp.int32, (8, B), 0)
    lane = lax.broadcasted_iota(jnp.int32, (8, B), 1)
    us, ws = [], []
    d = list(d)
    for s in range(8):
        lo = 16 * s
        inside = (lane >= lo) & (lane < lo + 16)
        pre = d[2 * s:2 * s + 2]
        nexts = range(2 * s + 2, min(16, 2 * s + 4))
        spread = [[lane_of(d[t], lo + j) for t in (2 * s, 2 * s + 1, *nexts)] for j in range(16)]
        cols = [tiles[:2] for tiles in spread]
        below = [[tiles[n + 2] for tiles in spread] for n in range(len(nexts))]
        own = [(lane - lo == row + 8 * r).astype(f32) for r in range(2)]
        x1 = [jnp.where(inside, own[r], pre[r]) for r in range(2)]
        x2 = [jnp.where(inside, pre[r], 0.0) for r in range(2)]
        snap1, snap2, piv = [None, None], [None, None], [None, None]
        for p in range(0, 16, 2):
            q = p + 1
            r, i, k = p // 8, p % 8, q % 8
            cp, cq = cols[p], cols[q]
            a, b, c = row_of(cp[r], i), row_of(cp[r], k), row_of(cq[r], k)
            det = a * c - b * b
            rd = recip(det)
            ba = b * recip(a)
            ca, cb, cc = c * rd, b * rd, a * rd
            isp, isq = row == i, row == k
            either = isp | isq
            ps = [cp[e] * ca - cq[e] * cb for e in range(2)]
            qs = [cq[e] * cc - cp[e] * cb for e in range(2)]
            ps[r] = jnp.where(isp, -ca, jnp.where(isq, cb, ps[r]))
            qs[r] = jnp.where(isp, cb, jnp.where(isq, -cc, qs[r]))

            def step(x):
                xp, xq = row_of(x[r], i), row_of(x[r], k)
                kept = [x[e] if e != r else jnp.where(either, 0.0, x[e]) for e in range(2)]
                return [kept[e] - (ps[e] * xp + qs[e] * xq) for e in range(2)], xp, xq

            for j in range(p + 2, 16):
                cols[j] = step(cols[j])[0]
            x1, xp, xq = step(x1)
            snap1[r] = jnp.where(isp, xp, jnp.where(isq, xq - ba * xp, 0.0 if snap1[r] is None else snap1[r]))
            x2, xp, xq = step(x2)
            snap2[r] = jnp.where(isp, xp, jnp.where(isq, xq - ba * xp, 0.0 if snap2[r] is None else snap2[r]))
            dd = jnp.where(isp, a, c - b * ba)
            piv[r] = dd if piv[r] is None else jnp.where(row >= i, dd, piv[r])
        for r in range(2):
            scale = lax.rsqrt(piv[r])
            w = snap1[r] * scale
            upper = jnp.where(inside & (lane - lo >= row + 8 * r), snap2[r] * scale, jnp.where(lane >= lo + 16, w, 0.0))
            us.append(upper)
            ws.append(jnp.where(lane < lo + 16, w, 0.0))
        if s == 7:
            break
        v = [row_of(x1[j // 8], j % 8) for j in range(16)]
        for n, t in enumerate(nexts):
            d[t] = jnp.where(inside, 0.0, d[t]) - tree([below[n][j] * v[j] for j in range(16)])
        if s < 6:
            rest = products_of(jnp.concatenate(pre, axis=0), jnp.concatenate(x1, axis=0))
            for t in range(2 * s + 4, 16):
                d[t] = jnp.where(inside, 0.0, d[t]) - rest[8 * t:8 * t + 8]
    return us, ws


def finish_kernel(gram_ref, s_hbm, basis_hbm, factor_ref, a_ref, w_ref, s_ref, o_ref, sem, osem):
    rows = s_ref.shape[0]
    load = pltpu.make_async_copy(s_hbm, s_ref, sem)
    load.start()
    eye = (lax.broadcasted_iota(jnp.int32, (B, B), 0) == lax.broadcasted_iota(jnp.int32, (B, B), 1))
    dl, ds_ = [], []
    tile_rows = {tile: slice(n * B, (n + 1) * B) for n, tile in enumerate(TILES)}
    for b in range(4):
        blk = jnp.where(eye, gram_ref[tile_rows[b, b], :], 0.0)
        dl.append(jnp.sum(blk, axis=0, keepdims=True))
        ds_.append(jnp.sum(blk, axis=1, keepdims=True))
    diag_l = jnp.concatenate(dl, axis=1)
    rs_l = lax.rsqrt(diag_l)
    sq_l = diag_l * rs_l
    for i, j in TILES:
        cols = slice(j * B, (j + 1) * B)
        a_ref[i * B:(i + 1) * B, cols] = gram_ref[tile_rows[i, j], :] * lax.rsqrt(ds_[i]) * rs_l[:, cols]
    for i in range(1, 4):
        a_ref[i * B:(i + 1) * B, :i * B] = jnp.zeros((B, i * B), f32)
    factor_ref[...] = jnp.zeros_like(factor_ref)

    for b in range(4):
        lo = b * B
        d = [a_ref[lo + 8 * i:lo + 8 * i + 8, lo:lo + B] for i in range(16)]
        us, ws = factor_block(d)
        for i in range(16):
            factor_ref[lo + 8 * i:lo + 8 * i + 8, lo:lo + B] = us[i] * sq_l[:, lo:lo + B]
            w_ref[lo + 8 * i:lo + 8 * i + 8, lo:lo + B] = ws[i]
        w = jnp.concatenate(ws, axis=0)
        panel = a_ref[lo:lo + B, :]
        pp = dot3(w, panel, ((1,), (0,)))
        if b > 0:
            w_ref[lo:lo + B, :lo] = pp[:, :lo]
        if b < 3:
            factor_ref[lo:lo + B, lo + B:] = pp[:, lo + B:] * sq_l[:, lo + B:]
            w_ref[lo:lo + B, lo + B:] = jnp.zeros((B, N - lo - B), f32)
            full = jnp.concatenate([pp[:, :lo], w, pp[:, lo + B:]], axis=1) if b > 0 else jnp.concatenate([w, pp[:, lo + B:]], axis=1)
            upd = dot3(pp[:, lo + B:], full, ((0,), (0,)))
            a_ref[lo + B:, lo:lo + B] = jnp.zeros((N - lo - B, B), f32)
            a_ref[lo + B:, :] = a_ref[lo + B:, :] - upd
    wh, wl = split(w_ref[...] * rs_l)
    dg = functools.partial(lax.dot_general, dimension_numbers=(((1,), (1,)), ((), ())), preferred_element_type=f32)
    load.wait()
    outs = []
    step = 256
    for i in range(rows // step):
        sl = slice(i * step, (i + 1) * step)
        sh, slo = split(s_ref[sl, :])
        for h in range(2):
            k = 256 * (h + 1)
            c = slice(256 * h, k)
            o_ref[sl, c] = dg(sh[:, :k], wh[c, :k]) + (dg(sh[:, :k], wl[c, :k]) + dg(slo[:, :k], wh[c, :k]))
        cp = pltpu.make_async_copy(o_ref.at[sl, :], basis_hbm.at[sl, :], osem.at[i])
        cp.start()
        outs.append(cp)
    for cp in outs:
        cp.wait()


def finish(gram, sketch):
    rows = sketch.shape[0]
    return pl.pallas_call(
        finish_kernel,
        out_shape=(jax.ShapeDtypeStruct((rows, N), f32), jax.ShapeDtypeStruct((N, N), f32)),
        in_specs=[pl.BlockSpec(memory_space=pltpu.VMEM), pl.BlockSpec(memory_space=pl.ANY)],
        out_specs=(pl.BlockSpec(memory_space=pl.ANY), pl.BlockSpec(memory_space=pltpu.VMEM)),
        scratch_shapes=[
            pltpu.VMEM((N, N), f32), pltpu.VMEM((N, N), f32), pltpu.VMEM((rows, N), f32), pltpu.VMEM((rows, N), f32),
            pltpu.SemaphoreType.DMA(()), pltpu.SemaphoreType.DMA((rows // 256,)),
        ],
        compiler_params=pltpu.CompilerParams(vmem_limit_bytes=64 * 2**20),
        name="finish",
    )(gram, sketch)


def positions():
    tm, u = lax.axis_index("tm"), lax.axis_index("units")
    return tm // 4, lax.rem(tm, 4), u // 2, lax.rem(u, 2)


def device(y, x, z, c):
    return (lax.rem(y, 4) * 4 + lax.rem(x, 4), lax.rem(z, 4) * 2 + lax.rem(c, 2))


PLANE = sorted(((dy, dx) for dy in range(4) for dx in range(4) if dy or dx),
               key=lambda o: -(min(o[0], 4 - o[0]) + min(o[1], 4 - o[1])))


def sketch_kernel(all_time, index_ref, x_hbm, values_hbm, sketch_hbm, gram_ref,
                  xbuf, values, wh, wl, part, from_core, far, far_in, near, near_in, share,
                  gram_core, plane, piece, pieces,
                  xsem, vsem, core_s, core_r, far_s, far_r, near_s, near_r, g2_s, g2_r, g3_s, g3_r,
                  g4_s, g4_r, g5_s, g5_r, sk_s, sk_r, fw_s, fw_r, own_sem):
    y, x, z, c = positions()
    me = y * 4 + x
    sibling = device(y, x, z, c + 1)
    up, down, across = device(y, x, z + 1, c), device(y, x, z + 3, c), device(y, x, z + 2, c)

    def remote(src, dst, ssem, rsem, to):
        return pltpu.make_async_remote_copy(src_ref=src, dst_ref=dst, send_sem=ssem, recv_sem=rsem,
                                            device_id=to, device_id_type=MESH)

    def inside(to):
        pl.semaphore_signal(pltpu.get_barrier_semaphore(), inc=1, device_id=to, device_id_type=MESH)

    groups = 4
    per = values.shape[0] // groups
    vloads = [pltpu.make_async_copy(values_hbm.at[pl.ds(g * per, per)], values.at[pl.ds(g * per, per)], vsem.at[g])
              for g in range(groups)]
    half = B // 2
    xloads = [[] for _ in range(4)]

    def fetch(t, to, row, count, n, cols=slice(None)):
        xloads[t].append(pltpu.make_async_copy(x_hbm.at[pl.ds(pl.multiple_of(row, half), count), cols],
                                               xbuf.at[t, pl.ds(to, count), cols], xsem.at[t, n]))

    for g in range(groups):
        fetch(0, 0, lax.rem(z + 2, 4) * 256, 256, g, pl.ds(g * per * B, per * B))
    for t in (1, 2):
        for n in range(4):
            target = lax.rem(z + (1, 3)[n % 2], 4)
            fetch(t, n * half, target * 256 + (n // 2) * B + (t - 1) * half, half, n)
    fetch(3, 0, z * 256, 256, 0)
    for g in range(groups):
        vloads[g].start()
        xloads[0][g].start()
    for to in (sibling, up, down, across):
        inside(to)
    for dy, dx in PLANE:
        inside(device(y + dy, x + dx, z, c))

    def product(t, k, begin=False):
        results = []
        for e in range(per):
            b = k * per + e
            rows = pl.ds(pl.multiple_of(b * B, B), B)
            if t == 0:
                h0, l0 = split(values[b, 0])
                h1, l1 = split(values[b, 1])
                high = jnp.concatenate([h0, h1], axis=1)
                low = jnp.concatenate([l0, l1], axis=1)
                wh[rows, :] = high
                wl[rows, :] = low
            else:
                high, low = wh[rows, :], wl[rows, :]
            xh, xl = split(xbuf[t, :, rows])
            dot = functools.partial(jnp.dot, preferred_element_type=f32)
            results.append(dot(jnp.concatenate([xh, xl], axis=1), jnp.concatenate([high, high], axis=0)) + dot(xh, low))
        for j in range(4):
            cols = slice(j * B, (j + 1) * B)
            total = 0.0 if begin else part[t, :, cols]
            for e in range(per):
                b = k * per + e
                total = total + jnp.where(index_ref[0, b] == j, results[e][:, :B],
                                          jnp.where(index_ref[1, b] == j, results[e][:, B:], 0.0))
            part[t, :, cols] = total

    def products(t, begin):
        def body(k, carry):
            product(t, k)
            return carry
        lax.fori_loop(begin, groups, body, 0)

    mine = pl.ds(pl.multiple_of(c * B, B), B)
    theirs = pl.ds(pl.multiple_of((1 - c) * B, B), B)
    core_cps = [remote(part.at[t, theirs, :], from_core.at[t], core_s.at[t], core_r.at[t], sibling) for t in range(4)]
    far_cps = [remote(far.at[pl.ds(d * half, half), :], far_in.at[d], far_s.at[d], far_r.at[d], (up, down)[d])
               for d in range(2)]
    near_cps = [[remote(near.at[h, d], near_in.at[h, d], near_s.at[h, d], near_r.at[h, d], (up, down)[d])
                 for d in range(2)] for h in range(2)]

    def both(t):
        core_cps[t].wait_recv()
        return part[t, mine, :] + from_core[t]

    for t in range(4):
        if t > 0:
            for cp in xloads[t]:
                cp.wait()
        if 0 < t < 3:
            for cp in xloads[t + 1]:
                cp.start()
        if t == 0:
            for g in range(groups):
                vloads[g].wait()
                xloads[0][g].wait()
                if g == 2:
                    for cp in xloads[1]:
                        cp.start()
                product(0, g, g == 0)
            pl.semaphore_wait(pltpu.get_barrier_semaphore(), 19)
        else:
            product(t, 0, True)
            s = both(t - 1)
            if t == 1:
                far[...] = s
                for cp in far_cps:
                    cp.start()
            else:
                h = t - 2
                far_cps[h].wait_recv()
                for d in range(2):
                    add = s[d * half:(d + 1) * half]
                    near[h, d] = add + far_in[h] if d == h else add
                    near_cps[h][d].start()
            products(t, 1)
        core_cps[t].start()
    own = both(3)
    for h in range(2):
        near_cps[h][0].wait_recv()
        near_cps[h][1].wait_recv()
        rows = slice(h * half, (h + 1) * half)
        share[pl.ds(pl.multiple_of(c * B + h * half, half), half), :] = own[rows] + near_in[h, 0] + near_in[h, 1]

    row0 = pl.multiple_of((z * 2 + c) * B, B)
    dest = sketch_hbm.at[pl.ds(row0, B), :]
    swap = remote(share.at[mine, :], share.at[mine, :], fw_s.at[0], fw_r.at[0], sibling)
    swap.start()
    sk = [remote(share.at[mine, :], dest, sk_s.at[i], sk_r.at[i], to) for i, to in enumerate((up, down, across))]
    sk[0].start()
    sk[1].start()
    swap.wait_recv()
    chip_rows = pl.ds(pl.multiple_of(z * 256, 256), 256)
    own_store = pltpu.make_async_copy(share, sketch_hbm.at[chip_rows, :], own_sem)
    own_store.start()

    tdot = functools.partial(lax.dot_general, dimension_numbers=(((0,), (0,)), ((), ())), preferred_element_type=f32)
    for n in range(5):
        (i0, j0), (i1, j1) = TILES[n], TILES[n + 5]
        i, j = jnp.where(c == 0, i0, i1), jnp.where(c == 0, j0, j1)
        ah, al = split(share[:, pl.ds(pl.multiple_of(i * B, B), B)])
        bh, bl = split(share[:, pl.ds(pl.multiple_of(j * B, B), B)])
        gram_core[n * B:(n + 1) * B, :] = tdot(ah, bh) + (tdot(ah, bl) + tdot(al, bh))

    core_half = 5 * B
    rows = core_half // 16

    def span(k):
        return pl.ds(pl.multiple_of(k * rows, 8), rows)

    scatters = []
    for n, (dy, dx) in enumerate(PLANE):
        to = device(y + dy, x + dx, z, c)
        scatters.append(remote(gram_core.at[span(to[0]), :], plane.at[me], g2_s.at[n], g2_r.at[n], to))
    for cp in scatters:
        cp.start()
    plane[me] = gram_core[span(me), :]
    for cp in scatters:
        cp.wait_recv()
    total = plane[0]
    for k in range(1, 16):
        total = total + plane[k]
    piece[...] = total
    pieces[z] = total
    g3 = [remote(piece, pieces.at[z], g3_s.at[i], g3_r.at[i], to) for i, to in enumerate((across, up, down))]
    for cp in g3:
        cp.start()
    sk[2].start()
    for cp in g3:
        cp.wait_recv()
    total = ((pieces[0] + pieces[1]) + (pieces[2] + pieces[3])) / all_time
    my_half = pl.ds(pl.multiple_of(c * core_half, core_half), core_half)
    my_rows = gram_ref.at[pl.ds(pl.multiple_of(c * core_half + me * rows, 8), rows), :]
    gram_ref[pl.ds(pl.multiple_of(c * core_half + me * rows, 8), rows), :] = total
    gathers = [remote(my_rows, my_rows, g4_s.at[n], g4_r.at[n], device(y + dy, x + dx, z, c))
               for n, (dy, dx) in enumerate(PLANE)]
    for cp in gathers:
        cp.start()
    forward = []
    for i, steps in ((0, 3), (1, 1), (2, 2)):
        sk[i].wait_recv()
        came = pl.multiple_of((lax.rem(z + steps, 4) * 2 + c) * B, B)
        block = sketch_hbm.at[pl.ds(came, B), :]
        cp = remote(block, block, fw_s.at[1 + i], fw_r.at[1 + i], sibling)
        cp.start()
        forward.append(cp)
    for cp in gathers:
        cp.wait_recv()
    g5 = remote(gram_ref.at[my_half, :], gram_ref.at[my_half, :], g5_s, g5_r, sibling)
    g5.start()
    for cp in (*core_cps, *far_cps, *near_cps[0], *near_cps[1], *g3, *sk, *scatters, *gathers, swap):
        cp.wait_send()
    own_store.wait()
    for cp in forward:
        cp.wait()
    g5.wait()


def sketch_and_gram(all_time, index, trajectory, values):
    rows, units = trajectory.shape
    dma = pltpu.SemaphoreType.DMA
    half = B // 2
    return pl.pallas_call(
        functools.partial(sketch_kernel, all_time),
        out_shape=(jax.ShapeDtypeStruct((rows, N), f32), jax.ShapeDtypeStruct((10 * B, B), f32)),
        in_specs=[pl.BlockSpec(memory_space=pltpu.SMEM), pl.BlockSpec(memory_space=pl.ANY), pl.BlockSpec(memory_space=pl.ANY)],
        out_specs=(pl.BlockSpec(memory_space=pl.ANY), pl.BlockSpec(memory_space=pltpu.VMEM)),
        scratch_shapes=[
            pltpu.VMEM((4, rows // 4, units), f32), pltpu.VMEM(values.shape, f32),
            pltpu.VMEM((units, 2 * B), bf16), pltpu.VMEM((units, 2 * B), bf16),
            pltpu.VMEM((4, rows // 4, N), f32), pltpu.VMEM((4, B, N), f32),
            pltpu.VMEM((B, N), f32), pltpu.VMEM((2, half, N), f32),
            pltpu.VMEM((2, 2, half, N), f32), pltpu.VMEM((2, 2, half, N), f32), pltpu.VMEM((2 * B, N), f32),
            pltpu.VMEM((5 * B, B), f32), pltpu.VMEM((16, 40, B), f32),
            pltpu.VMEM((40, B), f32), pltpu.VMEM((4, 40, B), f32),
            dma((4, 4)), dma((4,)), dma((4,)), dma((4,)), dma((2,)), dma((2,)), dma((2, 2)), dma((2, 2)),
            dma((16,)), dma((16,)), dma((3,)), dma((3,)), dma((16,)), dma((16,)), dma(()), dma(()),
            dma((3,)), dma((3,)), dma((4,)), dma((4,)), dma(()),
        ],
        compiler_params=pltpu.CompilerParams(collective_id=0, has_side_effects=True, vmem_limit_bytes=64 * 2**20),
        name="sketch_and_gram",
    )(index, trajectory, values)


def shards(trajectory, block_values, block_index):
    all_time = trajectory.shape[0] * lax.axis_size("tm")
    sketch, gram = sketch_and_gram(all_time, block_index.T, trajectory, block_values)
    return finish(gram, sketch)


def solution(mesh):
    return jax.shard_map(
        shards,
        mesh=mesh,
        in_specs=(P("tm", "units"), P("units", None, None, None), P("units", None)),
        out_specs=(P("tm", None), P()),
        check_vma=False,
    )
```

```python
import functools
import jax
import jax.numpy as jnp
from jax import lax
from jax.experimental import pallas as pl
from jax.experimental.pallas import tpu as pltpu
from jax.sharding import PartitionSpec as P

B = 128
N = 512
f32 = jnp.float32
bf16 = jnp.bfloat16
MESH = pl.DeviceIdType.MESH
TILES = [(i, j) for i in range(4) for j in range(i, 4)]


def split(x):
    hi = x.astype(bf16)
    return hi, (x - hi.astype(f32)).astype(bf16)


def dot3(a, b, dims):
    ah, al = split(a)
    bh, bl = split(b)
    dg = functools.partial(lax.dot_general, dimension_numbers=(dims, ((), ())), preferred_element_type=f32)
    return dg(ah, bh) + (dg(ah, bl) + dg(al, bh))


def row_of(x, p):
    return jnp.broadcast_to(x[p:p + 1, :], x.shape)


def lane_of(x, j):
    return jnp.broadcast_to(x[:, j:j + 1], x.shape)


def recip(x):
    return 1.0 / x


def three(x):
    high = x.astype(bf16).astype(f32)
    mid = (x - high).astype(bf16).astype(f32)
    return high, mid, x - high - mid


def products_of(a, b):
    ah, am, al = three(a)
    bh, bm, bl = three(b)
    a = jnp.concatenate([ah, ah, am, ah, al, am], axis=0).astype(bf16)
    b = jnp.concatenate([bh, bm, bh, bl, bh, bm], axis=0).astype(bf16)
    return lax.dot_general(a, b, (((0,), (0,)), ((), ())), preferred_element_type=f32)


def tree(terms):
    while len(terms) > 1:
        terms = [terms[i] + terms[i + 1] for i in range(0, len(terms), 2)]
    return terms[0]


def factor_block(d, between=None):
    row = lax.broadcasted_iota(jnp.int32, (8, B), 0)
    lane = lax.broadcasted_iota(jnp.int32, (8, B), 1)
    us, ws = [], []
    d = list(d)
    for s in range(8):
        lo = 16 * s
        inside = (lane >= lo) & (lane < lo + 16)
        pre = d[2 * s:2 * s + 2]
        nexts = range(2 * s + 2, min(16, 2 * s + 4))
        spread = [[lane_of(d[t], lo + j) for t in (2 * s, 2 * s + 1, *nexts)] for j in range(16)]
        cols = [tiles[:2] for tiles in spread]
        below = [[tiles[n + 2] for tiles in spread] for n in range(len(nexts))]
        own = [(lane - lo == row + 8 * r).astype(f32) for r in range(2)]
        x1 = [jnp.where(inside, own[r], pre[r]) for r in range(2)]
        x2 = [jnp.where(inside, pre[r], 0.0) for r in range(2)]
        snap1, snap2, piv = [None, None], [None, None], [None, None]
        for p in range(0, 16, 2):
            q = p + 1
            r, i, k = p // 8, p % 8, q % 8
            cp, cq = cols[p], cols[q]
            a, b, c = row_of(cp[r], i), row_of(cp[r], k), row_of(cq[r], k)
            det = a * c - b * b
            rd = recip(det)
            ba = b * recip(a)
            ca, cb, cc = c * rd, b * rd, a * rd
            isp, isq = row == i, row == k
            either = isp | isq
            ps = [cp[e] * ca - cq[e] * cb for e in range(2)]
            qs = [cq[e] * cc - cp[e] * cb for e in range(2)]
            ps[r] = jnp.where(isp, -ca, jnp.where(isq, cb, ps[r]))
            qs[r] = jnp.where(isp, cb, jnp.where(isq, -cc, qs[r]))

            def step(x):
                xp, xq = row_of(x[r], i), row_of(x[r], k)
                kept = [x[e] if e != r else jnp.where(either, 0.0, x[e]) for e in range(2)]
                return [kept[e] - (ps[e] * xp + qs[e] * xq) for e in range(2)], xp, xq

            for j in range(p + 2, 16):
                cols[j] = step(cols[j])[0]
            x1, xp, xq = step(x1)
            snap1[r] = jnp.where(isp, xp, jnp.where(isq, xq - ba * xp, 0.0 if snap1[r] is None else snap1[r]))
            x2, xp, xq = step(x2)
            snap2[r] = jnp.where(isp, xp, jnp.where(isq, xq - ba * xp, 0.0 if snap2[r] is None else snap2[r]))
            dd = jnp.where(isp, a, c - b * ba)
            piv[r] = dd if piv[r] is None else jnp.where(row >= i, dd, piv[r])
        for r in range(2):
            scale = lax.rsqrt(piv[r])
            w = snap1[r] * scale
            upper = jnp.where(inside & (lane - lo >= row + 8 * r), snap2[r] * scale, jnp.where(lane >= lo + 16, w, 0.0))
            us.append(upper)
            ws.append(jnp.where(lane < lo + 16, w, 0.0))
        if between is not None:
            between(s)
        if s == 7:
            break
        v = [row_of(x1[j // 8], j % 8) for j in range(16)]
        for n, t in enumerate(nexts):
            d[t] = jnp.where(inside, 0.0, d[t]) - tree([below[n][j] * v[j] for j in range(16)])
        if s < 6:
            rest = products_of(jnp.concatenate(pre, axis=0), jnp.concatenate(x1, axis=0))
            for t in range(2 * s + 4, 16):
                d[t] = jnp.where(inside, 0.0, d[t]) - rest[8 * t:8 * t + 8]
    return us, ws


def finish_kernel(gram_ref, s_hbm, basis_hbm, factor_ref, a_ref, w_ref, s_ref, o_ref, sem, osem):
    rows = s_ref.shape[0]
    load = pltpu.make_async_copy(s_hbm, s_ref, sem)
    load.start()
    eye = (lax.broadcasted_iota(jnp.int32, (B, B), 0) == lax.broadcasted_iota(jnp.int32, (B, B), 1))
    dl, ds_ = [], []
    tile_rows = {tile: slice(n * B, (n + 1) * B) for n, tile in enumerate(TILES)}
    for b in range(4):
        blk = jnp.where(eye, gram_ref[tile_rows[b, b], :], 0.0)
        dl.append(jnp.sum(blk, axis=0, keepdims=True))
        ds_.append(jnp.sum(blk, axis=1, keepdims=True))
    diag_l = jnp.concatenate(dl, axis=1)
    rs_l = lax.rsqrt(diag_l)
    sq_l = diag_l * rs_l
    for i, j in TILES:
        cols = slice(j * B, (j + 1) * B)
        a_ref[i * B:(i + 1) * B, cols] = gram_ref[tile_rows[i, j], :] * lax.rsqrt(ds_[i]) * rs_l[:, cols]
    for i in range(1, 4):
        a_ref[i * B:(i + 1) * B, :i * B] = jnp.zeros((B, i * B), f32)
    factor_ref[...] = jnp.zeros_like(factor_ref)

    dg = functools.partial(lax.dot_general, dimension_numbers=(((1,), (1,)), ((), ())), preferred_element_type=f32)
    step = 256
    chunks = [slice(i * step, (i + 1) * step) for i in range(rows // step)]

    def weights_of(h):
        k = 256 * (h + 1)
        return split(w_ref[256 * h:k, :k] * rs_l[:, :k])

    def columns(sl, h, weights):
        k = 256 * (h + 1)
        c = slice(256 * h, k)
        wh, wl = weights
        sh, slo = split(s_ref[sl, :k])
        o_ref[sl, c] = dg(sh, wh) + (dg(sh, wl) + dg(slo, wh))

    kept = []

    def left(s):
        if s == 0:
            load.wait()
            kept.append(weights_of(0))
        if s % 2 == 0:
            columns(chunks[s // 2], 0, kept[0])

    for b in range(4):
        lo = b * B
        d = [a_ref[lo + 8 * i:lo + 8 * i + 8, lo:lo + B] for i in range(16)]
        us, ws = factor_block(d, left if b == 3 else None)
        for i in range(16):
            factor_ref[lo + 8 * i:lo + 8 * i + 8, lo:lo + B] = us[i] * sq_l[:, lo:lo + B]
            w_ref[lo + 8 * i:lo + 8 * i + 8, lo:lo + B] = ws[i]
        w = jnp.concatenate(ws, axis=0)
        panel = a_ref[lo:lo + B, :]
        pp = dot3(w, panel, ((1,), (0,)))
        if b > 0:
            w_ref[lo:lo + B, :lo] = pp[:, :lo]
        if b < 3:
            factor_ref[lo:lo + B, lo + B:] = pp[:, lo + B:] * sq_l[:, lo + B:]
            w_ref[lo:lo + B, lo + B:] = jnp.zeros((B, N - lo - B), f32)
            full = jnp.concatenate([pp[:, :lo], w, pp[:, lo + B:]], axis=1) if b > 0 else jnp.concatenate([w, pp[:, lo + B:]], axis=1)
            upd = dot3(pp[:, lo + B:], full, ((0,), (0,)))
            a_ref[lo + B:, lo:lo + B] = jnp.zeros((N - lo - B, B), f32)
            a_ref[lo + B:, :] = a_ref[lo + B:, :] - upd
    outs = []
    weights = weights_of(1)
    for i, sl in enumerate(chunks):
        columns(sl, 1, weights)
        cp = pltpu.make_async_copy(o_ref.at[sl, :], basis_hbm.at[sl, :], osem.at[i])
        cp.start()
        outs.append(cp)
    for cp in outs:
        cp.wait()


def finish(gram, sketch):
    rows = sketch.shape[0]
    return pl.pallas_call(
        finish_kernel,
        out_shape=(jax.ShapeDtypeStruct((rows, N), f32), jax.ShapeDtypeStruct((N, N), f32)),
        in_specs=[pl.BlockSpec(memory_space=pltpu.VMEM), pl.BlockSpec(memory_space=pl.ANY)],
        out_specs=(pl.BlockSpec(memory_space=pl.ANY), pl.BlockSpec(memory_space=pltpu.VMEM)),
        scratch_shapes=[
            pltpu.VMEM((N, N), f32), pltpu.VMEM((N, N), f32), pltpu.VMEM((rows, N), f32), pltpu.VMEM((rows, N), f32),
            pltpu.SemaphoreType.DMA(()), pltpu.SemaphoreType.DMA((rows // 256,)),
        ],
        compiler_params=pltpu.CompilerParams(vmem_limit_bytes=64 * 2**20),
        name="finish",
    )(gram, sketch)


def positions():
    tm, u = lax.axis_index("tm"), lax.axis_index("units")
    return tm // 4, lax.rem(tm, 4), u // 2, lax.rem(u, 2)


def device(y, x, z, c):
    return (lax.rem(y, 4) * 4 + lax.rem(x, 4), lax.rem(z, 4) * 2 + lax.rem(c, 2))


PLANE = sorted(((dy, dx) for dy in range(4) for dx in range(4) if dy or dx),
               key=lambda o: -(min(o[0], 4 - o[0]) + min(o[1], 4 - o[1])))


def sketch_kernel(all_time, index_ref, x_hbm, values_hbm, sketch_hbm, gram_ref,
                  xbuf, values, wh, wl, part, from_core, far, far_in, near, near_in, share,
                  gram_core, plane, piece, pieces,
                  xsem, vsem, core_s, core_r, far_s, far_r, near_s, near_r, g2_s, g2_r, g3_s, g3_r,
                  g4_s, g4_r, g5_s, g5_r, sk_s, sk_r, fw_s, fw_r, own_sem):
    y, x, z, c = positions()
    me = y * 4 + x
    sibling = device(y, x, z, c + 1)
    up, down, across = device(y, x, z + 1, c), device(y, x, z + 3, c), device(y, x, z + 2, c)

    def remote(src, dst, ssem, rsem, to):
        return pltpu.make_async_remote_copy(src_ref=src, dst_ref=dst, send_sem=ssem, recv_sem=rsem,
                                            device_id=to, device_id_type=MESH)

    def inside(to):
        pl.semaphore_signal(pltpu.get_barrier_semaphore(), inc=1, device_id=to, device_id_type=MESH)

    groups = 4
    per = values.shape[0] // groups
    vloads = [pltpu.make_async_copy(values_hbm.at[pl.ds(g * per, per)], values.at[pl.ds(g * per, per)], vsem.at[g])
              for g in range(groups)]
    half = B // 2
    xloads = [[] for _ in range(4)]

    def fetch(t, to, row, count, n, cols=slice(None)):
        xloads[t].append(pltpu.make_async_copy(x_hbm.at[pl.ds(pl.multiple_of(row, half), count), cols],
                                               xbuf.at[t, pl.ds(to, count), cols], xsem.at[t, n]))

    for g in range(groups):
        fetch(0, 0, lax.rem(z + 2, 4) * 256, 256, g, pl.ds(g * per * B, per * B))
    for t in (1, 2):
        for n in range(4):
            target = lax.rem(z + (1, 3)[n % 2], 4)
            fetch(t, n * half, target * 256 + (n // 2) * B + (t - 1) * half, half, n)
    fetch(3, 0, z * 256, 256, 0)
    for g in range(groups):
        vloads[g].start()
        xloads[0][g].start()
    for to in (sibling, up, down, across):
        inside(to)
    for dy, dx in PLANE:
        inside(device(y + dy, x + dx, z, c))

    def product(t, k, begin=False):
        results = []
        for e in range(per):
            b = k * per + e
            rows = pl.ds(pl.multiple_of(b * B, B), B)
            if t == 0:
                h0, l0 = split(values[b, 0])
                h1, l1 = split(values[b, 1])
                high = jnp.concatenate([h0, h1], axis=1)
                low = jnp.concatenate([l0, l1], axis=1)
                wh[rows, :] = high
                wl[rows, :] = low
            else:
                high, low = wh[rows, :], wl[rows, :]
            xh, xl = split(xbuf[t, :, rows])
            dot = functools.partial(jnp.dot, preferred_element_type=f32)
            results.append(dot(jnp.concatenate([xh, xl], axis=1), jnp.concatenate([high, high], axis=0)) + dot(xh, low))
        for j in range(4):
            cols = slice(j * B, (j + 1) * B)
            total = 0.0 if begin else part[t, :, cols]
            for e in range(per):
                b = k * per + e
                total = total + jnp.where(index_ref[0, b] == j, results[e][:, :B],
                                          jnp.where(index_ref[1, b] == j, results[e][:, B:], 0.0))
            part[t, :, cols] = total

    def products(t, begin):
        def body(k, carry):
            product(t, k)
            return carry
        lax.fori_loop(begin, groups, body, 0)

    mine = pl.ds(pl.multiple_of(c * B, B), B)
    theirs = pl.ds(pl.multiple_of((1 - c) * B, B), B)
    core_cps = [remote(part.at[t, theirs, :], from_core.at[t], core_s.at[t], core_r.at[t], sibling) for t in range(4)]
    far_cps = [remote(far.at[h], far_in.at[h], far_s.at[h], far_r.at[h], across) for h in range(2)]
    near_cps = [[remote(near.at[h, d], near_in.at[h, d], near_s.at[h, d], near_r.at[h, d], (up, down)[d])
                 for d in range(2)] for h in range(2)]

    def both(t):
        core_cps[t].wait_recv()
        return part[t, mine, :] + from_core[t]

    for t in range(4):
        if t > 0:
            for cp in xloads[t]:
                cp.wait()
        if 0 < t < 3:
            for cp in xloads[t + 1]:
                cp.start()
        if t == 0:
            for g in range(groups):
                vloads[g].wait()
                xloads[0][g].wait()
                if g == 2:
                    for cp in xloads[1]:
                        cp.start()
                product(0, g, g == 0)
            pl.semaphore_wait(pltpu.get_barrier_semaphore(), 19)
        else:
            product(t, 0, True)
            s = both(t - 1)
            if t == 1:
                for h in range(2):
                    far[h] = s[h * half:(h + 1) * half]
                    far_cps[h].start()
            else:
                h = t - 2
                for d in range(2):
                    near[h, d] = s[d * half:(d + 1) * half]
                    near_cps[h][d].start()
            products(t, 1)
        core_cps[t].start()
    own = both(3)
    for h in range(2):
        far_cps[h].wait_recv()
        near_cps[h][0].wait_recv()
        near_cps[h][1].wait_recv()
        rows = slice(h * half, (h + 1) * half)
        share[pl.ds(pl.multiple_of(c * B + h * half, half), half), :] = (own[rows] + far_in[h]) + (near_in[h, 0] + near_in[h, 1])

    row0 = pl.multiple_of((z * 2 + c) * B, B)
    dest = sketch_hbm.at[pl.ds(row0, B), :]
    swap = remote(share.at[mine, :], share.at[mine, :], fw_s.at[0], fw_r.at[0], sibling)
    swap.start()
    sk = [remote(share.at[mine, :], dest, sk_s.at[i], sk_r.at[i], to) for i, to in enumerate((up, down, across))]
    sk[0].start()
    sk[1].start()
    tdot = functools.partial(lax.dot_general, dimension_numbers=(((0,), (0,)), ((), ())), preferred_element_type=f32)

    def tiles(rows):
        for n in range(5):
            (i0, j0), (i1, j1) = TILES[n], TILES[n + 5]
            i, j = jnp.where(c == 0, i0, i1), jnp.where(c == 0, j0, j1)
            ah, al = split(share[rows, pl.ds(pl.multiple_of(i * B, B), B)])
            bh, bl = split(share[rows, pl.ds(pl.multiple_of(j * B, B), B)])
            yield slice(n * B, (n + 1) * B), tdot(ah, bh) + (tdot(ah, bl) + tdot(al, bh))

    for at, tile in tiles(mine):
        gram_core[at, :] = tile
    swap.wait_recv()
    chip_rows = pl.ds(pl.multiple_of(z * 256, 256), 256)
    own_store = pltpu.make_async_copy(share, sketch_hbm.at[chip_rows, :], own_sem)
    own_store.start()
    for at, tile in tiles(theirs):
        gram_core[at, :] += tile

    core_half = 5 * B
    rows = core_half // 16

    def span(k):
        return pl.ds(pl.multiple_of(k * rows, 8), rows)

    scatters = []
    for n, (dy, dx) in enumerate(PLANE):
        to = device(y + dy, x + dx, z, c)
        scatters.append(remote(gram_core.at[span(to[0]), :], plane.at[me], g2_s.at[n], g2_r.at[n], to))
    for cp in scatters:
        cp.start()
    plane[me] = gram_core[span(me), :]
    for cp in scatters:
        cp.wait_recv()
    total = plane[0]
    for k in range(1, 16):
        total = total + plane[k]
    piece[...] = total
    pieces[z] = total
    g3 = [remote(piece, pieces.at[z], g3_s.at[i], g3_r.at[i], to) for i, to in enumerate((across, up, down))]
    for cp in g3:
        cp.start()
    sk[2].start()
    for cp in g3:
        cp.wait_recv()
    total = ((pieces[0] + pieces[1]) + (pieces[2] + pieces[3])) / all_time
    my_half = pl.ds(pl.multiple_of(c * core_half, core_half), core_half)
    my_rows = gram_ref.at[pl.ds(pl.multiple_of(c * core_half + me * rows, 8), rows), :]
    gram_ref[pl.ds(pl.multiple_of(c * core_half + me * rows, 8), rows), :] = total
    gathers = [remote(my_rows, my_rows, g4_s.at[n], g4_r.at[n], device(y + dy, x + dx, z, c))
               for n, (dy, dx) in enumerate(PLANE)]
    for cp in gathers:
        cp.start()
    forward = []
    for i, steps in ((0, 3), (1, 1), (2, 2)):
        sk[i].wait_recv()
        came = pl.multiple_of((lax.rem(z + steps, 4) * 2 + c) * B, B)
        block = sketch_hbm.at[pl.ds(came, B), :]
        cp = remote(block, block, fw_s.at[1 + i], fw_r.at[1 + i], sibling)
        cp.start()
        forward.append(cp)
    for cp in gathers:
        cp.wait_recv()
    g5 = remote(gram_ref.at[my_half, :], gram_ref.at[my_half, :], g5_s, g5_r, sibling)
    g5.start()
    for cp in (*core_cps, *far_cps, *near_cps[0], *near_cps[1], *g3, *sk, *scatters, *gathers, swap):
        cp.wait_send()
    own_store.wait()
    for cp in forward:
        cp.wait()
    g5.wait()


def sketch_and_gram(all_time, index, trajectory, values):
    rows, units = trajectory.shape
    dma = pltpu.SemaphoreType.DMA
    half = B // 2
    return pl.pallas_call(
        functools.partial(sketch_kernel, all_time),
        out_shape=(jax.ShapeDtypeStruct((rows, N), f32), jax.ShapeDtypeStruct((10 * B, B), f32)),
        in_specs=[pl.BlockSpec(memory_space=pltpu.SMEM), pl.BlockSpec(memory_space=pl.ANY), pl.BlockSpec(memory_space=pl.ANY)],
        out_specs=(pl.BlockSpec(memory_space=pl.ANY), pl.BlockSpec(memory_space=pltpu.VMEM)),
        scratch_shapes=[
            pltpu.VMEM((4, rows // 4, units), f32), pltpu.VMEM(values.shape, f32),
            pltpu.VMEM((units, 2 * B), bf16), pltpu.VMEM((units, 2 * B), bf16),
            pltpu.VMEM((4, rows // 4, N), f32), pltpu.VMEM((4, B, N), f32),
            pltpu.VMEM((2, half, N), f32), pltpu.VMEM((2, half, N), f32),
            pltpu.VMEM((2, 2, half, N), f32), pltpu.VMEM((2, 2, half, N), f32), pltpu.VMEM((2 * B, N), f32),
            pltpu.VMEM((5 * B, B), f32), pltpu.VMEM((16, 40, B), f32),
            pltpu.VMEM((40, B), f32), pltpu.VMEM((4, 40, B), f32),
            dma((4, 4)), dma((4,)), dma((4,)), dma((4,)), dma((2,)), dma((2,)), dma((2, 2)), dma((2, 2)),
            dma((16,)), dma((16,)), dma((3,)), dma((3,)), dma((16,)), dma((16,)), dma(()), dma(()),
            dma((3,)), dma((3,)), dma((4,)), dma((4,)), dma(()),
        ],
        compiler_params=pltpu.CompilerParams(collective_id=0, has_side_effects=True, vmem_limit_bytes=64 * 2**20),
        name="sketch_and_gram",
    )(index, trajectory, values)


def shards(trajectory, block_values, block_index):
    all_time = trajectory.shape[0] * lax.axis_size("tm")
    sketch, gram = sketch_and_gram(all_time, block_index.T, trajectory, block_values)
    return finish(gram, sketch)


def solution(mesh):
    return jax.shard_map(
        shards,
        mesh=mesh,
        in_specs=(P("tm", "units"), P("units", None, None, None), P("units", None)),
        out_specs=(P("tm", None), P()),
        check_vma=False,
    )
```

```python
import functools
import jax
import jax.numpy as jnp
from jax import lax
from jax.experimental import pallas as pl
from jax.experimental.pallas import tpu as pltpu
from jax.sharding import PartitionSpec as P

B = 128
N = 512
f32 = jnp.float32
bf16 = jnp.bfloat16
MESH = pl.DeviceIdType.MESH
TILES = [(i, j) for i in range(4) for j in range(i, 4)]


def split(x):
    hi = x.astype(bf16)
    return hi, (x - hi.astype(f32)).astype(bf16)


def dot3(a, b, dims):
    ah, al = split(a)
    bh, bl = split(b)
    dg = functools.partial(lax.dot_general, dimension_numbers=(dims, ((), ())), preferred_element_type=f32)
    return dg(ah, bh) + (dg(ah, bl) + dg(al, bh))


def row_of(x, p):
    return jnp.broadcast_to(x[p:p + 1, :], x.shape)


def lane_of(x, j):
    return jnp.broadcast_to(x[:, j:j + 1], x.shape)


def recip(x):
    return 1.0 / x


def three(x):
    high = x.astype(bf16).astype(f32)
    mid = (x - high).astype(bf16).astype(f32)
    return high, mid, x - high - mid


def products_of(a, b):
    ah, am, al = three(a)
    bh, bm, bl = three(b)
    a = jnp.concatenate([ah, ah, am, ah, al, am], axis=0).astype(bf16)
    b = jnp.concatenate([bh, bm, bh, bl, bh, bm], axis=0).astype(bf16)
    return lax.dot_general(a, b, (((0,), (0,)), ((), ())), preferred_element_type=f32)


def tree(terms):
    while len(terms) > 1:
        terms = [terms[i] + terms[i + 1] for i in range(0, len(terms), 2)]
    return terms[0]


def factor_block(d, between=None):
    row = lax.broadcasted_iota(jnp.int32, (8, B), 0)
    lane = lax.broadcasted_iota(jnp.int32, (8, B), 1)
    us, ws = [], []
    d = list(d)
    for s in range(8):
        lo = 16 * s
        inside = (lane >= lo) & (lane < lo + 16)
        pre = d[2 * s:2 * s + 2]
        nexts = range(2 * s + 2, min(16, 2 * s + 4))
        spread = [[lane_of(d[t], lo + j) for t in (2 * s, 2 * s + 1, *nexts)] for j in range(16)]
        cols = [tiles[:2] for tiles in spread]
        below = [[tiles[n + 2] for tiles in spread] for n in range(len(nexts))]
        own = [(lane - lo == row + 8 * r).astype(f32) for r in range(2)]
        x1 = [jnp.where(inside, own[r], pre[r]) for r in range(2)]
        x2 = [jnp.where(inside, pre[r], 0.0) for r in range(2)]
        snap1, snap2, piv = [None, None], [None, None], [None, None]
        for p in range(0, 16, 2):
            q = p + 1
            r, i, k = p // 8, p % 8, q % 8
            cp, cq = cols[p], cols[q]
            a, b, c = row_of(cp[r], i), row_of(cp[r], k), row_of(cq[r], k)
            det = a * c - b * b
            rd = recip(det)
            ba = b * recip(a)
            ca, cb, cc = c * rd, b * rd, a * rd
            isp, isq = row == i, row == k
            either = isp | isq
            ps = [cp[e] * ca - cq[e] * cb for e in range(2)]
            qs = [cq[e] * cc - cp[e] * cb for e in range(2)]
            ps[r] = jnp.where(isp, -ca, jnp.where(isq, cb, ps[r]))
            qs[r] = jnp.where(isp, cb, jnp.where(isq, -cc, qs[r]))

            def step(x):
                xp, xq = row_of(x[r], i), row_of(x[r], k)
                kept = [x[e] if e != r else jnp.where(either, 0.0, x[e]) for e in range(2)]
                return [kept[e] - (ps[e] * xp + qs[e] * xq) for e in range(2)], xp, xq

            for j in range(p + 2, 16):
                cols[j] = step(cols[j])[0]
            x1, xp, xq = step(x1)
            snap1[r] = jnp.where(isp, xp, jnp.where(isq, xq - ba * xp, 0.0 if snap1[r] is None else snap1[r]))
            x2, xp, xq = step(x2)
            snap2[r] = jnp.where(isp, xp, jnp.where(isq, xq - ba * xp, 0.0 if snap2[r] is None else snap2[r]))
            dd = jnp.where(isp, a, c - b * ba)
            piv[r] = dd if piv[r] is None else jnp.where(row >= i, dd, piv[r])
        for r in range(2):
            scale = lax.rsqrt(piv[r])
            w = snap1[r] * scale
            upper = jnp.where(inside & (lane - lo >= row + 8 * r), snap2[r] * scale, jnp.where(lane >= lo + 16, w, 0.0))
            us.append(upper)
            ws.append(jnp.where(lane < lo + 16, w, 0.0))
        if between is not None:
            between(s)
        if s == 7:
            break
        v = [row_of(x1[j // 8], j % 8) for j in range(16)]
        for n, t in enumerate(nexts):
            d[t] = jnp.where(inside, 0.0, d[t]) - tree([below[n][j] * v[j] for j in range(16)])
        if s < 6:
            rest = products_of(jnp.concatenate(pre, axis=0), jnp.concatenate(x1, axis=0))
            for t in range(2 * s + 4, 16):
                d[t] = jnp.where(inside, 0.0, d[t]) - rest[8 * t:8 * t + 8]
    return us, ws


def finish_kernel(gram_ref, s_hbm, basis_hbm, factor_ref, a_ref, w_ref, s_ref, o_ref, sem, osem):
    rows = s_ref.shape[0]
    load = pltpu.make_async_copy(s_hbm, s_ref, sem)
    load.start()
    eye = (lax.broadcasted_iota(jnp.int32, (B, B), 0) == lax.broadcasted_iota(jnp.int32, (B, B), 1))
    dl, ds_ = [], []
    tile_rows = {tile: slice(n * B, (n + 1) * B) for n, tile in enumerate(TILES)}
    for b in range(4):
        blk = jnp.where(eye, gram_ref[tile_rows[b, b], :], 0.0)
        dl.append(jnp.sum(blk, axis=0, keepdims=True))
        ds_.append(jnp.sum(blk, axis=1, keepdims=True))
    diag_l = jnp.concatenate(dl, axis=1)
    rs_l = lax.rsqrt(diag_l)
    sq_l = diag_l * rs_l
    for i, j in TILES:
        cols = slice(j * B, (j + 1) * B)
        a_ref[i * B:(i + 1) * B, cols] = gram_ref[tile_rows[i, j], :] * lax.rsqrt(ds_[i]) * rs_l[:, cols]
    for i in range(1, 4):
        a_ref[i * B:(i + 1) * B, :i * B] = jnp.zeros((B, i * B), f32)
    factor_ref[...] = jnp.zeros_like(factor_ref)

    dg = functools.partial(lax.dot_general, dimension_numbers=(((1,), (1,)), ((), ())), preferred_element_type=f32)
    step = 256
    chunks = [slice(i * step, (i + 1) * step) for i in range(rows // step)]

    def weights_of(h):
        k = 256 * (h + 1)
        return split(w_ref[256 * h:k, :k] * rs_l[:, :k])

    def columns(sl, h, weights):
        k = 256 * (h + 1)
        c = slice(256 * h, k)
        wh, wl = weights
        sh, slo = split(s_ref[sl, :k])
        o_ref[sl, c] = dg(sh, wh) + (dg(sh, wl) + dg(slo, wh))

    kept = []

    def left(s):
        if s == 0:
            load.wait()
            kept.append(weights_of(0))
        if s % 2 == 0:
            columns(chunks[s // 2], 0, kept[0])

    for b in range(4):
        lo = b * B
        d = [a_ref[lo + 8 * i:lo + 8 * i + 8, lo:lo + B] for i in range(16)]
        us, ws = factor_block(d, left if b == 3 else None)
        for i in range(16):
            factor_ref[lo + 8 * i:lo + 8 * i + 8, lo:lo + B] = us[i] * sq_l[:, lo:lo + B]
            w_ref[lo + 8 * i:lo + 8 * i + 8, lo:lo + B] = ws[i]
        w = jnp.concatenate(ws, axis=0)
        panel = a_ref[lo:lo + B, :]
        pp = dot3(w, panel, ((1,), (0,)))
        if b > 0:
            w_ref[lo:lo + B, :lo] = pp[:, :lo]
        if b < 3:
            factor_ref[lo:lo + B, lo + B:] = pp[:, lo + B:] * sq_l[:, lo + B:]
            w_ref[lo:lo + B, lo + B:] = jnp.zeros((B, N - lo - B), f32)
            full = jnp.concatenate([pp[:, :lo], w, pp[:, lo + B:]], axis=1) if b > 0 else jnp.concatenate([w, pp[:, lo + B:]], axis=1)
            upd = dot3(pp[:, lo + B:], full, ((0,), (0,)))
            a_ref[lo + B:, lo:lo + B] = jnp.zeros((N - lo - B, B), f32)
            a_ref[lo + B:, :] = a_ref[lo + B:, :] - upd
    outs = []
    weights = weights_of(1)
    for i, sl in enumerate(chunks):
        columns(sl, 1, weights)
        cp = pltpu.make_async_copy(o_ref.at[sl, :], basis_hbm.at[sl, :], osem.at[i])
        cp.start()
        outs.append(cp)
    for cp in outs:
        cp.wait()


def finish(gram, sketch):
    rows = sketch.shape[0]
    return pl.pallas_call(
        finish_kernel,
        out_shape=(jax.ShapeDtypeStruct((rows, N), f32), jax.ShapeDtypeStruct((N, N), f32)),
        in_specs=[pl.BlockSpec(memory_space=pltpu.VMEM), pl.BlockSpec(memory_space=pl.ANY)],
        out_specs=(pl.BlockSpec(memory_space=pl.ANY), pl.BlockSpec(memory_space=pltpu.VMEM)),
        scratch_shapes=[
            pltpu.VMEM((N, N), f32), pltpu.VMEM((N, N), f32), pltpu.VMEM((rows, N), f32), pltpu.VMEM((rows, N), f32),
            pltpu.SemaphoreType.DMA(()), pltpu.SemaphoreType.DMA((rows // 256,)),
        ],
        compiler_params=pltpu.CompilerParams(vmem_limit_bytes=64 * 2**20),
        name="finish",
    )(gram, sketch)


def positions():
    tm, u = lax.axis_index("tm"), lax.axis_index("units")
    return tm // 4, lax.rem(tm, 4), u // 2, lax.rem(u, 2)


def device(y, x, z, c):
    return (lax.rem(y, 4) * 4 + lax.rem(x, 4), lax.rem(z, 4) * 2 + lax.rem(c, 2))


PLANE = sorted(((dy, dx) for dy in range(4) for dx in range(4) if dy or dx),
               key=lambda o: -(min(o[0], 4 - o[0]) + min(o[1], 4 - o[1])))


def sketch_kernel(all_time, index_ref, x_hbm, values_hbm, sketch_hbm, gram_ref,
                  xbuf, values, wh, wl, part, from_core, far, far_in, near, near_in, share,
                  gram_core, plane, piece, pieces,
                  xsem, vsem, core_s, core_r, far_s, far_r, near_s, near_r, g2_s, g2_r, g3_s, g3_r,
                  g4_s, g4_r, g5_s, g5_r, sk_s, sk_r, fw_s, fw_r, own_sem):
    y, x, z, c = positions()
    me = y * 4 + x
    sibling = device(y, x, z, c + 1)
    up, down, across = device(y, x, z + 1, c), device(y, x, z + 3, c), device(y, x, z + 2, c)

    def remote(src, dst, ssem, rsem, to):
        return pltpu.make_async_remote_copy(src_ref=src, dst_ref=dst, send_sem=ssem, recv_sem=rsem,
                                            device_id=to, device_id_type=MESH)

    def inside(to):
        pl.semaphore_signal(pltpu.get_barrier_semaphore(), inc=1, device_id=to, device_id_type=MESH)

    groups = 4
    per = values.shape[0] // groups
    vloads = [pltpu.make_async_copy(values_hbm.at[pl.ds(g * per, per)], values.at[pl.ds(g * per, per)], vsem.at[g])
              for g in range(groups)]
    half = B // 2
    xloads = [[] for _ in range(4)]

    def fetch(t, to, row, count, n, cols=slice(None)):
        xloads[t].append(pltpu.make_async_copy(x_hbm.at[pl.ds(pl.multiple_of(row, half), count), cols],
                                               xbuf.at[t, pl.ds(to, count), cols], xsem.at[t, n]))

    for g in range(groups):
        fetch(0, 0, lax.rem(z + 2, 4) * 256, 256, g, pl.ds(g * per * B, per * B))
    for t in (1, 2):
        for n in range(4):
            target = lax.rem(z + (1, 3)[n % 2], 4)
            fetch(t, n * half, target * 256 + (n // 2) * B + (t - 1) * half, half, n)
    fetch(3, 0, z * 256, 256, 0)
    for g in range(groups):
        vloads[g].start()
        xloads[0][g].start()
    for to in (sibling, up, down, across):
        inside(to)
    for dy, dx in PLANE:
        inside(device(y + dy, x + dx, z, c))

    def product(t, k, begin=False):
        results = []
        for e in range(per):
            b = k * per + e
            rows = pl.ds(pl.multiple_of(b * B, B), B)
            if t == 0:
                h0, l0 = split(values[b, 0])
                h1, l1 = split(values[b, 1])
                high = jnp.concatenate([h0, h1], axis=1)
                low = jnp.concatenate([l0, l1], axis=1)
                wh[rows, :] = high
                wl[rows, :] = low
            else:
                high, low = wh[rows, :], wl[rows, :]
            xh, xl = split(xbuf[t, :, rows])
            dot = functools.partial(jnp.dot, preferred_element_type=f32)
            results.append(dot(jnp.concatenate([xh, xl], axis=1), jnp.concatenate([high, high], axis=0)) + dot(xh, low))
        for j in range(4):
            cols = slice(j * B, (j + 1) * B)
            total = 0.0 if begin else part[t, :, cols]
            for e in range(per):
                b = k * per + e
                total = total + jnp.where(index_ref[0, b] == j, results[e][:, :B],
                                          jnp.where(index_ref[1, b] == j, results[e][:, B:], 0.0))
            part[t, :, cols] = total

    def products(t, begin, end=groups):
        def body(k, carry):
            product(t, k)
            return carry
        lax.fori_loop(begin, end, body, 0)

    mine = pl.ds(pl.multiple_of(c * B, B), B)
    theirs = pl.ds(pl.multiple_of((1 - c) * B, B), B)
    core_cps = [remote(part.at[t, theirs, :], from_core.at[t], core_s.at[t], core_r.at[t], sibling) for t in range(4)]
    far_cps = [remote(far.at[h], far_in.at[h], far_s.at[h], far_r.at[h], (up, down)[h]) for h in range(2)]
    near_cps = [[remote(near.at[h, d], near_in.at[h, d], near_s.at[h, d], near_r.at[h, d], (up, down)[d])
                 for d in range(2)] for h in range(2)]

    def both(t):
        core_cps[t].wait_recv()
        return part[t, mine, :] + from_core[t]

    for t in range(4):
        if t > 0:
            for cp in xloads[t]:
                cp.wait()
        if 0 < t < 3:
            for cp in xloads[t + 1]:
                cp.start()
        if t == 0:
            for g in range(groups):
                vloads[g].wait()
                xloads[0][g].wait()
                if g == 2:
                    for cp in xloads[1]:
                        cp.start()
                product(0, g, g == 0)
            pl.semaphore_wait(pltpu.get_barrier_semaphore(), 19)
        else:
            product(t, 0, True)
            s = both(t - 1)
            if t == 1:
                for h in range(2):
                    far[h] = s[h * half:(h + 1) * half]
                    far_cps[h].start()
            else:
                h = t - 2
                for d in range(2):
                    add = s[d * half:(d + 1) * half]
                    if d == h == 1:
                        far_cps[1].wait_recv()
                        add = add + far_in[1]
                    near[h, d] = add
                    if d or h:
                        near_cps[h][d].start()
            if t == 2:
                products(2, 1, 3)
                far_cps[0].wait_recv()
                near[0, 0] += far_in[0]
                near_cps[0][0].start()
                products(2, 3)
            else:
                products(t, 1)
        core_cps[t].start()
    own = both(3)
    for h in range(2):
        near_cps[h][0].wait_recv()
        near_cps[h][1].wait_recv()
        rows = slice(h * half, (h + 1) * half)
        share[pl.ds(pl.multiple_of(c * B + h * half, half), half), :] = own[rows] + (near_in[h, 0] + near_in[h, 1])

    row0 = pl.multiple_of((z * 2 + c) * B, B)
    dest = sketch_hbm.at[pl.ds(row0, B), :]
    swap = remote(share.at[mine, :], share.at[mine, :], fw_s.at[0], fw_r.at[0], sibling)
    swap.start()
    sk = [remote(share.at[mine, :], dest, sk_s.at[i], sk_r.at[i], to) for i, to in enumerate((up, down))]
    for cp in sk:
        cp.start()
    tdot = functools.partial(lax.dot_general, dimension_numbers=(((0,), (0,)), ((), ())), preferred_element_type=f32)

    def tiles(rows):
        for n in range(5):
            (i0, j0), (i1, j1) = TILES[n], TILES[n + 5]
            i, j = jnp.where(c == 0, i0, i1), jnp.where(c == 0, j0, j1)
            ah, al = split(share[rows, pl.ds(pl.multiple_of(i * B, B), B)])
            bh, bl = split(share[rows, pl.ds(pl.multiple_of(j * B, B), B)])
            yield slice(n * B, (n + 1) * B), tdot(ah, bh) + (tdot(ah, bl) + tdot(al, bh))

    for at, tile in tiles(mine):
        gram_core[at, :] = tile
    swap.wait_recv()
    chip_rows = pl.ds(pl.multiple_of(z * 256, 256), 256)
    own_store = pltpu.make_async_copy(share, sketch_hbm.at[chip_rows, :], own_sem)
    own_store.start()
    for at, tile in tiles(theirs):
        gram_core[at, :] += tile

    core_half = 5 * B
    rows = core_half // 16

    def span(k):
        return pl.ds(pl.multiple_of(k * rows, 8), rows)

    scatters = []
    for n, (dy, dx) in enumerate(PLANE):
        to = device(y + dy, x + dx, z, c)
        scatters.append(remote(gram_core.at[span(to[0]), :], plane.at[me], g2_s.at[n], g2_r.at[n], to))
    for cp in scatters:
        cp.start()
    plane[me] = gram_core[span(me), :]
    for cp in scatters:
        cp.wait_recv()
    total = plane[0]
    for k in range(1, 16):
        total = total + plane[k]
    piece[...] = total
    pieces[z] = total
    g3 = [remote(piece, pieces.at[z], g3_s.at[i], g3_r.at[i], to) for i, to in enumerate((across, up, down))]
    for cp in g3:
        cp.start()
    forward = []

    def came(steps, first, count):
        row = pl.multiple_of((lax.rem(z + steps, 4) * 2 + c) * B + first, half)
        return sketch_hbm.at[pl.ds(row, count), :]

    def pass_on(steps, n):
        cp = remote(came(steps, 0, B), came(steps, 0, B), fw_s.at[n], fw_r.at[n], sibling)
        cp.start()
        forward.append(cp)

    relays = []
    for i, (steps, to) in enumerate(((3, up), (1, down))):
        sk[i].wait_recv()
        rows_on = came(steps, i * half, half)
        relays.append(remote(rows_on, rows_on, sk_s.at[2 + i], sk_r.at[2 + i], to))
        relays[i].start()
        pass_on(steps, 1 + i)
    for cp in g3:
        cp.wait_recv()
    total = ((pieces[0] + pieces[1]) + (pieces[2] + pieces[3])) / all_time
    my_half = pl.ds(pl.multiple_of(c * core_half, core_half), core_half)
    my_rows = gram_ref.at[pl.ds(pl.multiple_of(c * core_half + me * rows, 8), rows), :]
    gram_ref[pl.ds(pl.multiple_of(c * core_half + me * rows, 8), rows), :] = total
    gathers = [remote(my_rows, my_rows, g4_s.at[n], g4_r.at[n], device(y + dy, x + dx, z, c))
               for n, (dy, dx) in enumerate(PLANE)]
    for cp in gathers:
        cp.start()
    for cp in relays:
        cp.wait_recv()
    pass_on(2, 3)
    for cp in gathers:
        cp.wait_recv()
    g5 = remote(gram_ref.at[my_half, :], gram_ref.at[my_half, :], g5_s, g5_r, sibling)
    g5.start()
    for cp in (*core_cps, *far_cps, *near_cps[0], *near_cps[1], *g3, *sk, *relays, *scatters, *gathers, swap):
        cp.wait_send()
    own_store.wait()
    for cp in forward:
        cp.wait()
    g5.wait()


def sketch_and_gram(all_time, index, trajectory, values):
    rows, units = trajectory.shape
    dma = pltpu.SemaphoreType.DMA
    half = B // 2
    return pl.pallas_call(
        functools.partial(sketch_kernel, all_time),
        out_shape=(jax.ShapeDtypeStruct((rows, N), f32), jax.ShapeDtypeStruct((10 * B, B), f32)),
        in_specs=[pl.BlockSpec(memory_space=pltpu.SMEM), pl.BlockSpec(memory_space=pl.ANY), pl.BlockSpec(memory_space=pl.ANY)],
        out_specs=(pl.BlockSpec(memory_space=pl.ANY), pl.BlockSpec(memory_space=pltpu.VMEM)),
        scratch_shapes=[
            pltpu.VMEM((4, rows // 4, units), f32), pltpu.VMEM(values.shape, f32),
            pltpu.VMEM((units, 2 * B), bf16), pltpu.VMEM((units, 2 * B), bf16),
            pltpu.VMEM((4, rows // 4, N), f32), pltpu.VMEM((4, B, N), f32),
            pltpu.VMEM((2, half, N), f32), pltpu.VMEM((2, half, N), f32),
            pltpu.VMEM((2, 2, half, N), f32), pltpu.VMEM((2, 2, half, N), f32), pltpu.VMEM((2 * B, N), f32),
            pltpu.VMEM((5 * B, B), f32), pltpu.VMEM((16, 40, B), f32),
            pltpu.VMEM((40, B), f32), pltpu.VMEM((4, 40, B), f32),
            dma((4, 4)), dma((4,)), dma((4,)), dma((4,)), dma((2,)), dma((2,)), dma((2, 2)), dma((2, 2)),
            dma((16,)), dma((16,)), dma((3,)), dma((3,)), dma((16,)), dma((16,)), dma(()), dma(()),
            dma((4,)), dma((4,)), dma((4,)), dma((4,)), dma(()),
        ],
        compiler_params=pltpu.CompilerParams(collective_id=0, has_side_effects=True, vmem_limit_bytes=64 * 2**20),
        name="sketch_and_gram",
    )(index, trajectory, values)


def shards(trajectory, block_values, block_index):
    all_time = trajectory.shape[0] * lax.axis_size("tm")
    sketch, gram = sketch_and_gram(all_time, block_index.T, trajectory, block_values)
    return finish(gram, sketch)


def solution(mesh):
    return jax.shard_map(
        shards,
        mesh=mesh,
        in_specs=(P("tm", "units"), P("units", None, None, None), P("units", None)),
        out_specs=(P("tm", None), P()),
        check_vma=False,
    )
```

```python
import functools
import jax
import jax.numpy as jnp
from jax import lax
from jax.experimental import pallas as pl
from jax.experimental.pallas import tpu as pltpu
from jax.sharding import PartitionSpec as P

B = 128
N = 512
f32 = jnp.float32
bf16 = jnp.bfloat16
MESH = pl.DeviceIdType.MESH
TILES = [(i, j) for i in range(4) for j in range(i, 4)]


def split(x):
    hi = x.astype(bf16)
    return hi, (x - hi.astype(f32)).astype(bf16)


def dot3(a, b, dims):
    ah, al = split(a)
    bh, bl = split(b)
    dg = functools.partial(lax.dot_general, dimension_numbers=(dims, ((), ())), preferred_element_type=f32)
    return dg(ah, bh) + (dg(ah, bl) + dg(al, bh))


def row_of(x, p):
    return jnp.broadcast_to(x[p:p + 1, :], x.shape)


def lane_of(x, j):
    return jnp.broadcast_to(x[:, j:j + 1], x.shape)


def recip(x):
    return 1.0 / x


def three(x):
    high = x.astype(bf16).astype(f32)
    mid = (x - high).astype(bf16).astype(f32)
    return high, mid, x - high - mid


def products_of(a, b):
    ah, am, al = three(a)
    bh, bm, bl = three(b)
    a = jnp.concatenate([ah, ah, am, ah, al, am], axis=0).astype(bf16)
    b = jnp.concatenate([bh, bm, bh, bl, bh, bm], axis=0).astype(bf16)
    return lax.dot_general(a, b, (((0,), (0,)), ((), ())), preferred_element_type=f32)


def tree(terms):
    while len(terms) > 1:
        terms = [terms[i] + terms[i + 1] for i in range(0, len(terms), 2)]
    return terms[0]


def factor_block(d, between=None):
    row = lax.broadcasted_iota(jnp.int32, (8, B), 0)
    lane = lax.broadcasted_iota(jnp.int32, (8, B), 1)
    us, ws = [], []
    d = list(d)
    for s in range(8):
        lo = 16 * s
        inside = (lane >= lo) & (lane < lo + 16)
        pre = d[2 * s:2 * s + 2]
        nexts = range(2 * s + 2, min(16, 2 * s + 4))
        spread = [[lane_of(d[t], lo + j) for t in (2 * s, 2 * s + 1, *nexts)] for j in range(16)]
        cols = [tiles[:2] for tiles in spread]
        below = [[tiles[n + 2] for tiles in spread] for n in range(len(nexts))]
        own = [(lane - lo == row + 8 * r).astype(f32) for r in range(2)]
        x1 = [jnp.where(inside, own[r], pre[r]) for r in range(2)]
        x2 = [jnp.where(inside, pre[r], 0.0) for r in range(2)]
        snap1, snap2, piv = [None, None], [None, None], [None, None]
        for p in range(0, 16, 2):
            q = p + 1
            r, i, k = p // 8, p % 8, q % 8
            cp, cq = cols[p], cols[q]
            a, b, c = row_of(cp[r], i), row_of(cp[r], k), row_of(cq[r], k)
            det = a * c - b * b
            rd = recip(det)
            ba = b * recip(a)
            ca, cb, cc = c * rd, b * rd, a * rd
            isp, isq = row == i, row == k
            either = isp | isq
            ps = [cp[e] * ca - cq[e] * cb for e in range(2)]
            qs = [cq[e] * cc - cp[e] * cb for e in range(2)]
            ps[r] = jnp.where(isp, -ca, jnp.where(isq, cb, ps[r]))
            qs[r] = jnp.where(isp, cb, jnp.where(isq, -cc, qs[r]))

            def step(x):
                xp, xq = row_of(x[r], i), row_of(x[r], k)
                kept = [x[e] if e != r else jnp.where(either, 0.0, x[e]) for e in range(2)]
                return [kept[e] - (ps[e] * xp + qs[e] * xq) for e in range(2)], xp, xq

            for j in range(p + 2, 16):
                cols[j] = step(cols[j])[0]
            x1, xp, xq = step(x1)
            snap1[r] = jnp.where(isp, xp, jnp.where(isq, xq - ba * xp, 0.0 if snap1[r] is None else snap1[r]))
            x2, xp, xq = step(x2)
            snap2[r] = jnp.where(isp, xp, jnp.where(isq, xq - ba * xp, 0.0 if snap2[r] is None else snap2[r]))
            dd = jnp.where(isp, a, c - b * ba)
            piv[r] = dd if piv[r] is None else jnp.where(row >= i, dd, piv[r])
        for r in range(2):
            scale = lax.rsqrt(piv[r])
            w = snap1[r] * scale
            upper = jnp.where(inside & (lane - lo >= row + 8 * r), snap2[r] * scale, jnp.where(lane >= lo + 16, w, 0.0))
            us.append(upper)
            ws.append(jnp.where(lane < lo + 16, w, 0.0))
        if between is not None:
            between(s)
        if s == 7:
            break
        v = [row_of(x1[j // 8], j % 8) for j in range(16)]
        for n, t in enumerate(nexts):
            d[t] = jnp.where(inside, 0.0, d[t]) - tree([below[n][j] * v[j] for j in range(16)])
        if s < 6:
            rest = products_of(jnp.concatenate(pre, axis=0), jnp.concatenate(x1, axis=0))
            for t in range(2 * s + 4, 16):
                d[t] = jnp.where(inside, 0.0, d[t]) - rest[8 * t:8 * t + 8]
    return us, ws


def finish_kernel(gram_ref, s_hbm, basis_hbm, factor_ref, a_ref, w_ref, s_ref, o_ref, sem, osem):
    rows = s_ref.shape[0]
    load = pltpu.make_async_copy(s_hbm, s_ref, sem)
    load.start()
    eye = (lax.broadcasted_iota(jnp.int32, (B, B), 0) == lax.broadcasted_iota(jnp.int32, (B, B), 1))
    dl, ds_ = [], []
    tile_rows = {tile: slice(n * B, (n + 1) * B) for n, tile in enumerate(TILES)}
    for b in range(4):
        blk = jnp.where(eye, gram_ref[tile_rows[b, b], :], 0.0)
        dl.append(jnp.sum(blk, axis=0, keepdims=True))
        ds_.append(jnp.sum(blk, axis=1, keepdims=True))
    diag_l = jnp.concatenate(dl, axis=1)
    rs_l = lax.rsqrt(diag_l)
    sq_l = diag_l * rs_l
    for i, j in TILES:
        cols = slice(j * B, (j + 1) * B)
        a_ref[i * B:(i + 1) * B, cols] = gram_ref[tile_rows[i, j], :] * lax.rsqrt(ds_[i]) * rs_l[:, cols]
    for i in range(1, 4):
        a_ref[i * B:(i + 1) * B, :i * B] = jnp.zeros((B, i * B), f32)
    factor_ref[...] = jnp.zeros_like(factor_ref)

    dg = functools.partial(lax.dot_general, dimension_numbers=(((1,), (1,)), ((), ())), preferred_element_type=f32)
    step = 256
    chunks = [slice(i * step, (i + 1) * step) for i in range(rows // step)]

    def weights_of(h):
        k = 256 * (h + 1)
        return split(w_ref[256 * h:k, :k] * rs_l[:, :k])

    def columns(sl, h, weights):
        k = 256 * (h + 1)
        c = slice(256 * h, k)
        wh, wl = weights
        sh, slo = split(s_ref[sl, :k])
        o_ref[sl, c] = dg(sh, wh) + (dg(sh, wl) + dg(slo, wh))

    kept = []

    def left(s):
        if s == 0:
            load.wait()
            kept.append(weights_of(0))
        if s % 2 == 0:
            columns(chunks[s // 2], 0, kept[0])

    for b in range(4):
        lo = b * B
        d = [a_ref[lo + 8 * i:lo + 8 * i + 8, lo:lo + B] for i in range(16)]
        us, ws = factor_block(d, left if b == 3 else None)
        for i in range(16):
            factor_ref[lo + 8 * i:lo + 8 * i + 8, lo:lo + B] = us[i] * sq_l[:, lo:lo + B]
            w_ref[lo + 8 * i:lo + 8 * i + 8, lo:lo + B] = ws[i]
        w = jnp.concatenate(ws, axis=0)
        panel = a_ref[lo:lo + B, :]
        pp = dot3(w, panel, ((1,), (0,)))
        if b > 0:
            w_ref[lo:lo + B, :lo] = pp[:, :lo]
        if b < 3:
            factor_ref[lo:lo + B, lo + B:] = pp[:, lo + B:] * sq_l[:, lo + B:]
            w_ref[lo:lo + B, lo + B:] = jnp.zeros((B, N - lo - B), f32)
            full = jnp.concatenate([pp[:, :lo], w, pp[:, lo + B:]], axis=1) if b > 0 else jnp.concatenate([w, pp[:, lo + B:]], axis=1)
            upd = dot3(pp[:, lo + B:], full, ((0,), (0,)))
            a_ref[lo + B:, lo:lo + B] = jnp.zeros((N - lo - B, B), f32)
            a_ref[lo + B:, :] = a_ref[lo + B:, :] - upd
    outs = []
    weights = weights_of(1)
    for i, sl in enumerate(chunks):
        columns(sl, 1, weights)
        cp = pltpu.make_async_copy(o_ref.at[sl, :], basis_hbm.at[sl, :], osem.at[i])
        cp.start()
        outs.append(cp)
    for cp in outs:
        cp.wait()


def finish(gram, sketch):
    rows = sketch.shape[0]
    return pl.pallas_call(
        finish_kernel,
        out_shape=(jax.ShapeDtypeStruct((rows, N), f32), jax.ShapeDtypeStruct((N, N), f32)),
        in_specs=[pl.BlockSpec(memory_space=pltpu.VMEM), pl.BlockSpec(memory_space=pl.ANY)],
        out_specs=(pl.BlockSpec(memory_space=pl.ANY), pl.BlockSpec(memory_space=pltpu.VMEM)),
        scratch_shapes=[
            pltpu.VMEM((N, N), f32), pltpu.VMEM((N, N), f32), pltpu.VMEM((rows, N), f32), pltpu.VMEM((rows, N), f32),
            pltpu.SemaphoreType.DMA(()), pltpu.SemaphoreType.DMA((rows // 256,)),
        ],
        compiler_params=pltpu.CompilerParams(vmem_limit_bytes=64 * 2**20),
        name="finish",
    )(gram, sketch)


def positions():
    tm, u = lax.axis_index("tm"), lax.axis_index("units")
    return tm // 4, lax.rem(tm, 4), u // 2, lax.rem(u, 2)


def device(y, x, z, c):
    return (lax.rem(y, 4) * 4 + lax.rem(x, 4), lax.rem(z, 4) * 2 + lax.rem(c, 2))


PLANE = sorted(((dy, dx) for dy in range(4) for dx in range(4) if dy or dx),
               key=lambda o: -(min(o[0], 4 - o[0]) + min(o[1], 4 - o[1])))


def sketch_kernel(all_time, index_ref, x_hbm, values_hbm, sketch_hbm, gram_ref,
                  xbuf, values, wh, wl, part, from_core, far, far_in, near, near_in, share,
                  turned, gram_core, plane, piece, pieces,
                  xsem, vsem, core_s, core_r, far_s, far_r, near_s, near_r, g2_s, g2_r, g3_s, g3_r,
                  g4_s, g4_r, g5_s, g5_r, sk_s, sk_r, fw_s, fw_r, own_sem):
    y, x, z, c = positions()
    me = y * 4 + x
    sibling = device(y, x, z, c + 1)
    up, down, across = device(y, x, z + 1, c), device(y, x, z + 3, c), device(y, x, z + 2, c)

    def remote(src, dst, ssem, rsem, to):
        return pltpu.make_async_remote_copy(src_ref=src, dst_ref=dst, send_sem=ssem, recv_sem=rsem,
                                            device_id=to, device_id_type=MESH)

    def inside(to):
        pl.semaphore_signal(pltpu.get_barrier_semaphore(), inc=1, device_id=to, device_id_type=MESH)

    groups = 4
    per = values.shape[0] // groups
    vloads = [pltpu.make_async_copy(values_hbm.at[pl.ds(g * per, per)], values.at[pl.ds(g * per, per)], vsem.at[g])
              for g in range(groups)]
    half = B // 2
    xloads = [[] for _ in range(4)]

    def fetch(t, to, row, count, n, cols=slice(None)):
        xloads[t].append(pltpu.make_async_copy(x_hbm.at[pl.ds(pl.multiple_of(row, half), count), cols],
                                               xbuf.at[t, pl.ds(to, count), cols], xsem.at[t, n]))

    for g in range(groups):
        fetch(0, 0, lax.rem(z + 2, 4) * 256, 256, g, pl.ds(g * per * B, per * B))
    for t in (1, 2):
        for n in range(4):
            target = lax.rem(z + (1, 3)[n % 2], 4)
            fetch(t, n * half, target * 256 + (n // 2) * B + (t - 1) * half, half, n)
    fetch(3, 0, z * 256, 256, 0)
    for g in range(groups):
        vloads[g].start()
        xloads[0][g].start()
    for to in (sibling, up, down, across):
        inside(to)
    for dy, dx in PLANE:
        inside(device(y + dy, x + dx, z, c))

    def product(t, k, begin=False):
        results = []
        for e in range(per):
            b = k * per + e
            rows = pl.ds(pl.multiple_of(b * B, B), B)
            if t == 0:
                h0, l0 = split(values[b, 0])
                h1, l1 = split(values[b, 1])
                high = jnp.concatenate([h0, h1], axis=1)
                low = jnp.concatenate([l0, l1], axis=1)
                wh[rows, :] = high
                wl[rows, :] = low
            else:
                high, low = wh[rows, :], wl[rows, :]
            xh, xl = split(xbuf[t, :, rows])
            dot = functools.partial(jnp.dot, preferred_element_type=f32)
            results.append(dot(jnp.concatenate([xh, xl], axis=1), jnp.concatenate([high, high], axis=0)) + dot(xh, low))
        for j in range(4):
            cols = slice(j * B, (j + 1) * B)
            total = 0.0 if begin else part[t, :, cols]
            for e in range(per):
                b = k * per + e
                total = total + jnp.where(index_ref[0, b] == j, results[e][:, :B],
                                          jnp.where(index_ref[1, b] == j, results[e][:, B:], 0.0))
            part[t, :, cols] = total

    def products(t, begin, end=groups):
        def body(k, carry):
            product(t, k)
            return carry
        lax.fori_loop(begin, end, body, 0)

    mine = pl.ds(pl.multiple_of(c * B, B), B)
    theirs = pl.ds(pl.multiple_of((1 - c) * B, B), B)
    core_cps = [remote(part.at[t, theirs, :], from_core.at[t], core_s.at[t], core_r.at[t], sibling) for t in range(4)]
    far_cps = [remote(far.at[h], far_in.at[h], far_s.at[h], far_r.at[h], (up, down)[h]) for h in range(2)]
    near_cps = [[remote(near.at[h, d], near_in.at[h, d], near_s.at[h, d], near_r.at[h, d], (up, down)[d])
                 for d in range(2)] for h in range(2)]

    def both(t):
        core_cps[t].wait_recv()
        return part[t, mine, :] + from_core[t]

    for t in range(4):
        if t > 0:
            for cp in xloads[t]:
                cp.wait()
        if 0 < t < 3:
            for cp in xloads[t + 1]:
                cp.start()
        if t == 0:
            for g in range(groups):
                vloads[g].wait()
                xloads[0][g].wait()
                if g == 2:
                    for cp in xloads[1]:
                        cp.start()
                product(0, g, g == 0)
            pl.semaphore_wait(pltpu.get_barrier_semaphore(), 19)
        else:
            product(t, 0, True)
            s = both(t - 1)
            if t == 1:
                for h in range(2):
                    far[h] = s[h * half:(h + 1) * half]
                    far_cps[h].start()
            else:
                h = t - 2
                for d in range(2):
                    add = s[d * half:(d + 1) * half]
                    if d == h == 1:
                        far_cps[1].wait_recv()
                        add = add + far_in[1]
                    near[h, d] = add
                    if d or h:
                        near_cps[h][d].start()
            if t == 2:
                products(2, 1, 3)
                far_cps[0].wait_recv()
                near[0, 0] += far_in[0]
                near_cps[0][0].start()
                products(2, 3)
            else:
                products(t, 1)
        core_cps[t].start()
    own = both(3)
    for h in range(2):
        near_cps[h][0].wait_recv()
        near_cps[h][1].wait_recv()
        rows = slice(h * half, (h + 1) * half)
        share[pl.ds(pl.multiple_of(c * B + h * half, half), half), :] = own[rows] + (near_in[h, 0] + near_in[h, 1])

    row0 = pl.multiple_of((z * 2 + c) * B, B)
    dest = sketch_hbm.at[pl.ds(row0, B), :]
    swap = remote(share.at[mine, :], share.at[mine, :], fw_s.at[0], fw_r.at[0], sibling)
    swap.start()
    sk = [remote(share.at[mine, :], dest, sk_s.at[i], sk_r.at[i], to) for i, to in enumerate((up, down))]
    dot = functools.partial(jnp.dot, preferred_element_type=f32)

    def tiles(rows):
        for i in range(4):
            turned[i * B:(i + 1) * B, :] = share[rows, i * B:(i + 1) * B].T
        for n in range(5):
            (i0, j0), (i1, j1) = TILES[n], TILES[n + 5]
            i, j = jnp.where(c == 0, i0, i1), jnp.where(c == 0, j0, j1)
            ah, al = split(turned[pl.ds(pl.multiple_of(i * B, B), B), :])
            bh, bl = split(share[rows, pl.ds(pl.multiple_of(j * B, B), B)])
            yield slice(n * B, (n + 1) * B), dot(ah, bh) + (dot(ah, bl) + dot(al, bh))

    for at, tile in tiles(mine):
        gram_core[at, :] = tile
    swap.wait_recv()
    chip_rows = pl.ds(pl.multiple_of(z * 256, 256), 256)
    own_store = pltpu.make_async_copy(share, sketch_hbm.at[chip_rows, :], own_sem)
    own_store.start()
    for at, tile in tiles(theirs):
        gram_core[at, :] += tile

    core_half = 5 * B
    rows = core_half // 16

    def span(k):
        return pl.ds(pl.multiple_of(k * rows, 8), rows)

    scatters = []
    for n, (dy, dx) in enumerate(PLANE):
        to = device(y + dy, x + dx, z, c)
        scatters.append(remote(gram_core.at[span(to[0]), :], plane.at[me], g2_s.at[n], g2_r.at[n], to))
    for cp in scatters:
        cp.start()
    for cp in sk:
        cp.start()
    plane[me] = gram_core[span(me), :]
    for cp in scatters:
        cp.wait_recv()
    total = plane[0]
    for k in range(1, 16):
        total = total + plane[k]
    piece[...] = total
    pieces[z] = total
    g3 = [remote(piece, pieces.at[z], g3_s.at[i], g3_r.at[i], to) for i, to in enumerate((across, up, down))]
    for cp in g3:
        cp.start()
    forward = []

    def came(steps, first, count):
        row = pl.multiple_of((lax.rem(z + steps, 4) * 2 + c) * B + first, half)
        return sketch_hbm.at[pl.ds(row, count), :]

    def pass_on(steps, n):
        cp = remote(came(steps, 0, B), came(steps, 0, B), fw_s.at[n], fw_r.at[n], sibling)
        cp.start()
        forward.append(cp)

    relays = []
    for i, (steps, to) in enumerate(((3, up), (1, down))):
        sk[i].wait_recv()
        rows_on = came(steps, i * half, half)
        relays.append(remote(rows_on, rows_on, sk_s.at[2 + i], sk_r.at[2 + i], to))
        relays[i].start()
        pass_on(steps, 1 + i)
    for cp in g3:
        cp.wait_recv()
    total = ((pieces[0] + pieces[1]) + (pieces[2] + pieces[3])) / all_time
    my_rows = gram_ref.at[pl.ds(pl.multiple_of(c * core_half + me * rows, 8), rows), :]
    gram_ref[pl.ds(pl.multiple_of(c * core_half + me * rows, 8), rows), :] = total
    gathers = [remote(my_rows, my_rows, g4_s.at[n], g4_r.at[n], device(y + dy, x + dx, z, c))
               for n, (dy, dx) in enumerate(PLANE)]
    for cp in gathers:
        cp.start()
    for cp in relays:
        cp.wait_recv()
    pass_on(2, 3)
    halves = [remote(my_rows, my_rows, g5_s.at[15], g5_r.at[15], sibling)]
    halves[0].start()
    for n, (dy, dx) in reversed(list(enumerate(PLANE))):
        gathers[n].wait_recv()
        source = lax.rem(y + 4 - dy, 4) * 4 + lax.rem(x + 4 - dx, 4)
        block = gram_ref.at[pl.ds(pl.multiple_of(c * core_half + source * rows, 8), rows), :]
        halves.append(remote(block, block, g5_s.at[n], g5_r.at[n], sibling))
        halves[-1].start()
    for cp in (*core_cps, *far_cps, *near_cps[0], *near_cps[1], *g3, *sk, *relays, *scatters, *gathers, swap):
        cp.wait_send()
    own_store.wait()
    for cp in forward:
        cp.wait()
    for cp in halves:
        cp.wait()


def sketch_and_gram(all_time, index, trajectory, values):
    rows, units = trajectory.shape
    dma = pltpu.SemaphoreType.DMA
    half = B // 2
    return pl.pallas_call(
        functools.partial(sketch_kernel, all_time),
        out_shape=(jax.ShapeDtypeStruct((rows, N), f32), jax.ShapeDtypeStruct((10 * B, B), f32)),
        in_specs=[pl.BlockSpec(memory_space=pltpu.SMEM), pl.BlockSpec(memory_space=pl.ANY), pl.BlockSpec(memory_space=pl.ANY)],
        out_specs=(pl.BlockSpec(memory_space=pl.ANY), pl.BlockSpec(memory_space=pltpu.VMEM)),
        scratch_shapes=[
            pltpu.VMEM((4, rows // 4, units), f32), pltpu.VMEM(values.shape, f32),
            pltpu.VMEM((units, 2 * B), bf16), pltpu.VMEM((units, 2 * B), bf16),
            pltpu.VMEM((4, rows // 4, N), f32), pltpu.VMEM((4, B, N), f32),
            pltpu.VMEM((2, half, N), f32), pltpu.VMEM((2, half, N), f32),
            pltpu.VMEM((2, 2, half, N), f32), pltpu.VMEM((2, 2, half, N), f32), pltpu.VMEM((2 * B, N), f32),
            pltpu.VMEM((N, B), f32), pltpu.VMEM((5 * B, B), f32), pltpu.VMEM((16, 40, B), f32),
            pltpu.VMEM((40, B), f32), pltpu.VMEM((4, 40, B), f32),
            dma((4, 4)), dma((4,)), dma((4,)), dma((4,)), dma((2,)), dma((2,)), dma((2, 2)), dma((2, 2)),
            dma((16,)), dma((16,)), dma((3,)), dma((3,)), dma((16,)), dma((16,)), dma((16,)), dma((16,)),
            dma((4,)), dma((4,)), dma((4,)), dma((4,)), dma(()),
        ],
        compiler_params=pltpu.CompilerParams(collective_id=0, has_side_effects=True, vmem_limit_bytes=64 * 2**20),
        name="sketch_and_gram",
    )(index, trajectory, values)


def shards(trajectory, block_values, block_index):
    all_time = trajectory.shape[0] * lax.axis_size("tm")
    sketch, gram = sketch_and_gram(all_time, block_index.T, trajectory, block_values)
    return finish(gram, sketch)


def solution(mesh):
    return jax.shard_map(
        shards,
        mesh=mesh,
        in_specs=(P("tm", "units"), P("units", None, None, None), P("units", None)),
        out_specs=(P("tm", None), P()),
        check_vma=False,
    )
```
